512 devices in a mesh: width: 16 (over z, core), hidden: 32 (over y, x).
Axes of the slice: x: 4, y: 8, z: 8, core: 2. Of those that a mesh axis runs over, the one named last changes fastest.
Arguments:
- tokens: bfloat16 [2, 512, 18432], P(None, 'hidden', 'width'), may hold values from -1000 to 1000
- gain: float32 [18432], P('width'), may hold values from 0.5 to 2
- query_weight: bfloat16 [18432, 12288], P('width', 'hidden'), may hold values from -0.063570226 to 0.063570226
- keyval_weight: bfloat16 [18432, 512], P('width', 'hidden'), may hold values from -0.046875 to 0.046875
- out_weight: bfloat16 [12288, 18432], P('hidden', 'width'), may hold values from -0.0546875 to 0.0546875
- key_cache: bfloat16 [512, 2048, 256], P(('hidden', 'width')), may hold values from -8 to 8
- value_cache: bfloat16 [512, 2048, 256], P(('hidden', 'width')), may hold values from -6 to 6
- lengths: int32 [512], P(('hidden', 'width')), may hold values from 2 to 2048, as said below
Outputs:
- attn_out: bfloat16 [2, 512, 18432], P(None, 'hidden', 'width')
The draws below stay inside these ranges and needn't reach their ends.
Inputs may be any that keep to these rules, and one draw needn't show every extreme that they name: `lengths`: every row attends to at least two cached positions; some row attends to all 2048.
All inputs are finite; a program needn't handle non-finite values.
Results may differ from the reference program's by a relative error of at most 0.04.
Values may be sent and summed in bfloat16 or wider, within the bound.
A program may use at most 64 MiB of HBM per device.

```python
import math
import jax
import jax.numpy as jnp
from jax import lax

D = 18432
HEADS = 48
HEAD_DIM = 256
CACHE = 2048
STEPS = 2
FEAT = 12288
FEAT_DEV = 384
ROWS = 512
N_HIDDEN = 32


def draw_tokens(key, part):
    key = jax.random.fold_in(key, 1)
    key_base = jax.random.fold_in(key, 0)
    key_rows = jax.random.fold_in(key, 1)
    key_cols = jax.random.fold_in(key, 2)
    key_offset = jax.random.fold_in(key, 4)
    row_scale = jnp.exp(jax.random.uniform(key_rows, (STEPS, ROWS, 1), jnp.float32) * math.log(10.0))
    position = jnp.arange(D, dtype=jnp.float32) / (D - 1)
    offset = jnp.clip(jax.random.normal(key_offset, (STEPS, ROWS, 1), jnp.float32), -2.0, 2.0)
    rough = jnp.exp(jax.random.uniform(key_cols, (1, 1, D), jnp.float32) * math.log(2.0))
    col_scale = jnp.exp(position * math.log(10.0))[None, None, :] * rough
    base = jnp.clip(jax.random.normal(key_base, (STEPS, ROWS, D), jnp.float32), -3.0, 3.0)
    return ((base + 0.5 * offset) * row_scale * col_scale).astype(jnp.bfloat16)


def draw_query_weight(key, part):
    key = jax.random.fold_in(key, 2)
    key_base = jax.random.fold_in(key, 0)
    return (jnp.clip(jax.random.normal(key_base, (D, HEADS * HEAD_DIM), jnp.float32), -3.0, 3.0) / math.sqrt(D)).astype(jnp.bfloat16)


def draw_key_cache(key, part):
    key = jax.random.fold_in(key, 3)
    return jnp.clip(2.0 * jax.random.normal(key, (ROWS, CACHE, HEAD_DIM), jnp.float32), -8.0, 8.0).astype(jnp.bfloat16)


def draw_lengths(key, part):
    key = jax.random.fold_in(key, 4)
    key_len, key_pick = jax.random.split(key, 2)
    drawn = jax.random.randint(key_len, (ROWS,), 2, CACHE + 1, dtype=jnp.int32)
    chosen = jax.random.randint(key_pick, (), 0, ROWS, dtype=jnp.int32)
    return drawn.at[chosen].set(CACHE)


def steps_of(stream_key, extent, cuts, least, largest):
    loudness = 1.0
    for axis_at, shards_of in cuts:
        draws = jax.random.uniform(jax.random.fold_in(jax.random.fold_in(stream_key, 6), axis_at), (shards_of,), jnp.float32, least / len(cuts), largest / len(cuts))
        loudness = loudness * jnp.repeat(jnp.exp(draws), extent[axis_at] // shards_of).reshape((-1,) + (1,) * (len(extent) - 1 - axis_at))
    return loudness


def bell_draw(key, shape, scale, reach, cuts=(), held_as=jnp.bfloat16):
    values = scale * jax.random.normal(key, shape, jnp.float32)
    if cuts:
        values = values * steps_of(key, shape, cuts, -0.22, 0.18)
    return jnp.clip(values, -reach, reach).astype(held_as)


def setup_inputs(seed: int = 0) -> dict:
    key_of = jax.random.split(jax.random.key(seed), 9)
    return {
        "tokens": draw_tokens(jax.random.fold_in(key_of[8], 71), 0),
        "gain": jnp.clip(jnp.exp(math.log(2.0) - 1.3862944 * jax.random.uniform(key_of[1], (D,), jnp.float32) ** steps_of(key_of[1], (D,), ((0, 16),), -0.2, 0.2)), 0.5, 2.0),
        "query_weight": draw_query_weight(jax.random.fold_in(key_of[8], 71), 0),
        "keyval_weight": bell_draw(key_of[3], (D, 2 * HEAD_DIM), D ** -0.5, 0.046875, ((0, 16), (1, 32))),
        "out_weight": bell_draw(key_of[4], (FEAT, D), FEAT ** -0.5, 0.0546875, ((0, 32), (1, 16))),
        "key_cache": draw_key_cache(jax.random.fold_in(key_of[8], 71), 0),
        "value_cache": bell_draw(key_of[6], (ROWS, CACHE, HEAD_DIM), 1.0, 6.0, ((0, 512),)),
        "lengths": draw_lengths(jax.random.fold_in(key_of[8], 71), 0),
    }


EPS = 1e-05
MASKED_SCORE = -1e+30

def attend_row(inputs):
    query_row, keys_row, values_row, usable_row, new_keys, new_values = inputs
    inv_root = HEAD_DIM ** (-0.5)
    cached_scores = jnp.dot(query_row, keys_row.T, preferred_element_type=jnp.float32) * inv_root
    cached_scores = jnp.where(usable_row[None, :], cached_scores, MASKED_SCORE)
    fresh_scores = jnp.dot(query_row, new_keys.T, preferred_element_type=jnp.float32) * inv_root
    row_peak = jnp.maximum(lax.optimization_barrier(jnp.max(cached_scores, axis=1)), lax.optimization_barrier(jnp.max(fresh_scores, axis=1)))
    cached_weights = jnp.where(usable_row[None, :], jnp.exp(cached_scores - row_peak[:, None]), 0.0)
    fresh_weights = jnp.exp(fresh_scores - row_peak[:, None])
    weight_total = lax.optimization_barrier(jnp.sum(cached_weights, axis=1)) + lax.optimization_barrier(jnp.sum(fresh_weights, axis=1))
    weighted = jnp.dot(cached_weights.astype(jnp.bfloat16), values_row, preferred_element_type=jnp.float32)
    weighted = weighted + jnp.dot(fresh_weights.astype(jnp.bfloat16), new_values, preferred_element_type=jnp.float32)
    return (weighted / weight_total[:, None]).astype(jnp.bfloat16)

def add_block(running, block_pair):
    partial_term = jnp.dot(block_pair[0], block_pair[1], preferred_element_type=jnp.float32).astype(jnp.bfloat16)
    partial_term = lax.optimization_barrier(partial_term)
    return (running + partial_term.astype(jnp.float32), None)

def reference(tokens, gain, query_weight, keyval_weight, out_weight, key_cache, value_cache, lengths):
    usable = jnp.arange(CACHE, dtype=jnp.int32)[None, :] < lengths[:, None]
    keys_new = []
    values_new = []
    results = []
    for decode_step in range(STEPS):
        values = tokens[decode_step].astype(jnp.float32)
        average = lax.optimization_barrier(jnp.mean(values, axis=1, keepdims=True))
        centered = values - average
        spread = lax.optimization_barrier(jnp.mean(centered * centered, axis=1, keepdims=True))
        normed = (centered * lax.rsqrt(spread + EPS) * gain[None, :]).astype(jnp.bfloat16)
        queries = jnp.dot(normed, query_weight, preferred_element_type=jnp.float32).astype(jnp.bfloat16)
        keyval = jnp.dot(normed, keyval_weight, preferred_element_type=jnp.float32).astype(jnp.bfloat16)
        keys_new.append(keyval[:, :HEAD_DIM])
        values_new.append(keyval[:, HEAD_DIM:])
        stacked_keys = jnp.stack(keys_new, axis=1)
        stacked_values = jnp.stack(values_new, axis=1)
        queries = queries.reshape(ROWS, HEADS, HEAD_DIM)
        attended = lax.map(attend_row, (queries, key_cache, value_cache, usable, stacked_keys, stacked_values))
        attended = attended.reshape(ROWS, FEAT)
        blocks_att = attended.reshape(ROWS, N_HIDDEN, FEAT_DEV).transpose(1, 0, 2)
        blocks_weight = out_weight.reshape(N_HIDDEN, FEAT_DEV, D)
        summed, unused = lax.scan(add_block, jnp.zeros((ROWS, D), jnp.float32), (blocks_att, blocks_weight))
        results.append(summed.astype(jnp.bfloat16))
    return jnp.stack(results, axis=0)
```

```python
import jax
import jax.numpy as jnp
from jax import lax
from jax.experimental import pallas as pl
from jax.experimental.pallas import tpu as pltpu
from jax.sharding import PartitionSpec as P

MESH = pl.DeviceIdType.MESH
F32, BF16 = jnp.float32, jnp.bfloat16

D = 18432
HEADS = 48
HEAD_DIM = 256
CACHE = 2048
FEAT_DEV = 384
WIDTH_DEV = 1152
WIDTH_CHIP = 2304
JOINT = 512
EPS = 1e-05
MASKED_SCORE = -1e30

X, Y, Z = 4, 8, 8
CUT = 1024
REST = WIDTH_CHIP - CUT
ORDER = (0, 1, 7, 2, 6, 3, 5, 4)
POS = {ry: pos for pos, ry in enumerate(ORDER)}
BY_DISTANCE = ((0,), (1, 7), (2, 6), (3, 5), (4,))
CHUNKS = ((0, 3), (3, 5), (5, 7), (7, 8))

SENDS = 340
ARRIVALS = 340


class Links:
    def __init__(self, send_sems, recv_sems):
        self.send_sems = send_sems
        self.recv_sems = recv_sems
        self.sent = []
        self.keys = {}
        self.h = lax.axis_index("hidden")
        self.w = lax.axis_index("width")
        self.y, self.x = lax.div(self.h, X), lax.rem(self.h, X)
        self.z, self.c = lax.div(self.w, 2), lax.rem(self.w, 2)

    def hidden(self, ry, rx):
        return lax.rem(self.y + ry, Y) * X + lax.rem(self.x + rx, X)

    def width(self, rz, rc):
        return lax.rem(self.z + rz, Z) * 2 + self.core(rc)

    def core(self, rc):
        return self.c if rc == 0 else 1 - self.c

    def device(self, ry=0, rx=0, rz=0, rc=0):
        return {"hidden": self.hidden(ry % Y, rx % X), "width": self.width(rz % Z, rc)}

    def arrival(self, key):
        return self.recv_sems.at[self.keys.setdefault(key, len(self.keys))]

    def push(self, src, dst, to, key):
        copy = pltpu.make_async_remote_copy(
            src_ref=src,
            dst_ref=dst,
            send_sem=self.send_sems.at[len(self.sent)],
            recv_sem=self.arrival(key),
            device_id=self.device(**to),
            device_id_type=MESH,
        )
        copy.start()
        self.sent.append(copy)

    def arrive(self, dst, key):
        pltpu.make_async_remote_copy(
            src_ref=dst,
            dst_ref=dst,
            send_sem=self.send_sems.at[0],
            recv_sem=self.arrival(key),
            device_id=self.device(rc=1),
            device_id_type=MESH,
        ).wait_recv()

    def finish(self):
        for copy in self.sent:
            copy.wait_send()


def iota(shape, axis):
    return lax.broadcasted_iota(jnp.int32, shape, axis)


def kernel(tokens, gain, lengths, query_weight, keyval_weight, out_weight, key_cache, value_cache, out, s):
    links = Links(s["send_sems"], s["recv_sems"])
    c, z, h, w = links.c, links.z, links.h, links.w
    width_peers = [(rz, rc) for rz in (4, 3, 5, 2, 6, 1, 7, 0) for rc in (0, 1) if (rz, rc) != (0, 0)]
    hidden_peers = [(ry, rx) for ry in reversed(ORDER) for rx in (2, 1, 3, 0) if (ry, rx) != (0, 0)]

    joint, out_w = s["joint"], s["out_w"]
    mine = pl.ds(pl.multiple_of(c * WIDTH_DEV, WIDTH_DEV), WIDTH_DEV)
    local = s["local_sems"]
    loads = [
        pltpu.make_async_copy(keyval_weight, s["keyval_w"], local.at[0]),
        pltpu.make_async_copy(query_weight, joint.at[mine, pl.ds(0, FEAT_DEV)], local.at[1]),
        pltpu.make_async_copy(out_weight, out_w.at[c], local.at[2]),
        pltpu.make_async_copy(key_cache.at[0], s["keys"], local.at[3]),
        pltpu.make_async_copy(value_cache.at[0], s["values"], local.at[4]),
    ]
    for load in loads:
        load.start()

    barrier = pltpu.get_barrier_semaphore()
    for rz, rc in width_peers:
        pl.semaphore_signal(barrier, inc=1, device_id=links.device(rz=rz, rc=rc), device_id_type=MESH)
    for ry, rx in hidden_peers:
        pl.semaphore_signal(barrier, inc=1, device_id=links.device(ry=ry, rx=rx), device_id_type=MESH)

    rows = tokens[...].astype(F32).reshape(32, WIDTH_DEV)
    own_mean = jnp.sum(rows, axis=1, keepdims=True) * (1.0 / WIDTH_DEV)
    centered = rows - own_mean
    own_spread = jnp.sum(centered * centered, axis=1, keepdims=True)
    diagonal = iota((32, 128), 0) == iota((32, 128), 1)
    mean_lanes = jnp.sum(jnp.where(diagonal, own_mean, 0.0), axis=0, keepdims=True)
    spread_lanes = jnp.sum(jnp.where(diagonal, own_spread, 0.0), axis=0, keepdims=True)
    stats = s["stats"]
    stats[0] = jnp.where(iota((8, 128), 0) == 0, mean_lanes, spread_lanes)
    gains = s["gains"]
    gains[c] = jnp.broadcast_to(gain[...], (8, WIDTH_DEV))
    halves = s["halves"]
    halves[c] = tokens[c]

    pl.semaphore_wait(barrier, len(width_peers) + len(hidden_peers))

    for rz, rc in width_peers:
        slot = ((-rz) % Z) * 2 + rc
        links.push(stats.at[0], stats.at[slot], dict(rz=rz, rc=rc), ("stats", slot))
    links.push(tokens.at[1 - c], halves.at[c], dict(rc=1), "halves")
    links.push(gains.at[c], gains.at[c], dict(rc=1), "gains")
    loads[0].wait()
    joint[mine, FEAT_DEV:JOINT] = jnp.concatenate(
        [s["keyval_w"][...], jnp.zeros((WIDTH_DEV, JOINT - FEAT_DEV - 16), BF16)], axis=1
    )
    loads[1].wait()
    links.push(joint.at[mine], joint.at[mine], dict(rc=1), "joint")
    loads[2].wait()

    for rz, rc in width_peers:
        slot = rz * 2 + rc
        links.arrive(stats.at[slot], ("stats", slot))
    gathered = stats[...]
    mean = jnp.sum(gathered, axis=0) * (1.0 / 16)
    apart = gathered - mean[None]
    first = iota((8, 128), 0) == 0
    spread = jnp.sum(jnp.where(first[None], WIDTH_DEV * (apart * apart), gathered), axis=0)
    scale = lax.rsqrt((spread[0:1] + spread[1:2]) * (1.0 / D) + EPS)
    here = iota((16, 128), 1) == iota((16, 128), 0) + c * 16
    row_mean = jnp.sum(jnp.where(here, mean[0:1], 0.0), axis=1, keepdims=True)
    row_scale = jnp.sum(jnp.where(here, scale, 0.0), axis=1, keepdims=True)
    links.arrive(halves.at[1 - c], "halves")
    links.arrive(gains.at[1 - c], "gains")
    normed = [
        ((halves[half].astype(F32) - row_mean) * row_scale * gains[half, 0:1]).astype(BF16) for half in (0, 1)
    ]
    ga, gb = s["ga"], s["gb"]
    ga[0, 0] = normed[0][:, :CUT]
    gb[0, 0] = jnp.concatenate([normed[0][:, CUT:], normed[1]], axis=1)

    def a_along_y(ry, rx, up):
        to = (ry - 1) % Y if up else (ry + 1) % Y
        if to == 4 and up != (rx < 2):
            return
        links.push(ga.at[POS[ry], rx], ga.at[POS[to], rx], dict(ry=1 if up else -1), ("a", to, rx))

    def b_along_y(ry, up):
        to = (ry - 1) % Y if up else (ry + 1) % Y
        if to == 4 and not up:
            return
        links.push(gb.at[POS[ry], 0], gb.at[POS[to], 0], dict(ry=1 if up else -1), ("b", to, 0))

    def b_along_x(ry, rx, right):
        to = (rx - 1) % X if right else (rx + 1) % X
        links.push(gb.at[POS[ry], rx], gb.at[POS[ry], to], dict(rx=1 if right else -1), ("b", ry, to))

    def a_from(ry, rx):
        links.arrive(ga.at[POS[ry], rx], ("a", ry, rx))

    def b_from(ry, rx):
        links.arrive(gb.at[POS[ry], rx], ("b", ry, rx))

    acc, spread_out, packed, shares = s["acc"], s["spread_out"], s["packed"], s["shares"]
    owned, owned_sum, queries = s["owned"], s["owned_sum"], s["queries"]

    def project(chunk):
        p0, p1 = CHUNKS[chunk]
        count = p1 - p0
        if chunk == 0:
            links.arrive(joint.at[pl.ds(pl.multiple_of((1 - c) * WIDTH_DEV, WIDTH_DEV), WIDTH_DEV)], "joint")
        partial = jnp.dot(
            ga[p0:p1].reshape(count * 64, CUT), joint[0:CUT], preferred_element_type=F32
        ) + jnp.dot(gb[p0:p1].reshape(count * 64, REST), joint[CUT:WIDTH_CHIP], preferred_element_type=F32)
        for k in range(4):
            acc[k, p0 * 64 : p1 * 64] = partial[:, k * 128 : (k + 1) * 128]
        span = slice(p0 * 16, p1 * 16)
        for row in range(16):
            for k in range(4):
                spread_out[row, pl.ds(p0 * 16 + k, count * 4, stride=4), :] = acc[
                    k, pl.ds(p0 * 64 + row, count * 4, stride=16), :
                ]
            packed[row, span] = spread_out[row, span].astype(BF16)
        part = pl.ds(p0 * 16, count * 16)
        for rz, rc in width_peers:
            links.push(
                packed.at[links.width(rz, rc), part],
                shares.at[c, (-rz) % Z, part],
                dict(rz=rz, rc=rc),
                ("shares", chunk, (-rz) % Z, rc),
            )
        shares[c, 0, span] = packed[w, span]

    def hand_out(chunk):
        p0, p1 = CHUNKS[chunk]
        count = p1 - p0
        span = slice(p0 * 16, p1 * 16)
        for rz, rc in width_peers:
            links.arrive(shares.at[links.core(rc), rz, pl.ds(p0 * 16, count * 16)], ("shares", chunk, rz, rc))
        for step in range(2):
            total = shares[step, 0, span].astype(F32)
            for rz in range(1, Z):
                total = total + shares[step, rz, span].astype(F32)
            owned_sum[step, span] = total
            for k in range(4):
                owned[pl.ds(p0 * 32 + step * 4 + k, count * 4, stride=8), :] = owned_sum[
                    step, pl.ds(p0 * 16 + k, count * 4, stride=4), :
                ]
        here_h = pl.ds(pl.multiple_of(h * 8, 8), 8)
        for pos in range(p0, p1):
            ry = ORDER[pos]
            for rx in range(X):
                tile = pl.ds((pos * X + rx) * 8, 8)
                if (ry, rx) == (0, 0):
                    queries[here_h] = owned[tile]
                else:
                    links.push(
                        owned.at[tile],
                        queries.at[here_h],
                        dict(ry=ry, rx=rx),
                        ("queries", (-ry) % Y, (-rx) % X),
                    )

    for rx in (1, 3, 2):
        links.push(ga.at[0, 0], ga.at[0, (-rx) % X], dict(rx=rx), ("a", 0, (-rx) % X))
    for up in (True, False):
        b_along_y(0, up)
        a_along_y(0, 0, up)
    for right in (True, False):
        b_along_x(0, 0, right)
    links.push(out_w.at[c], out_w.at[c], dict(rc=1), "out_w")
    for rx in (1, 3, 2):
        a_from(0, rx)
        for up in (True, False):
            a_along_y(0, rx, up)

    def b_second(distance):
        for ry in BY_DISTANCE[distance]:
            b_from(ry, 1)
            if POS[ry] % 2 == 1:
                b_along_x(ry, 1, False)
            b_from(ry, 3)
            if POS[ry] % 2 == 0:
                b_along_x(ry, 3, True)

    def b_third(distance):
        for ry in BY_DISTANCE[distance]:
            b_from(ry, 2)

    for distance in range(1, 5):
        for ry in BY_DISTANCE[distance]:
            b_from(ry, 0)
            if ry >= 5:
                b_along_y(ry, True)
            if ry <= 3:
                b_along_y(ry, False)
            for right in (True, False):
                b_along_x(ry, 0, right)
        b_second(distance - 1)
        for ry in BY_DISTANCE[distance]:
            for rx in range(X):
                a_from(ry, rx)
                if ry >= 5:
                    a_along_y(ry, rx, True)
                if ry <= 3:
                    a_along_y(ry, rx, False)
        if distance >= 2:
            b_third(distance - 2)
        if distance >= 3:
            project(distance - 3)
        if distance >= 4:
            hand_out(distance - 4)
    b_second(4)
    b_third(3)
    project(2)
    hand_out(1)
    b_third(4)
    project(3)
    hand_out(2)
    hand_out(3)

    for ry, rx in hidden_peers:
        links.arrive(
            queries.at[pl.ds(pl.multiple_of(links.hidden(ry, rx) * 8, 8), 8)], ("queries", ry, rx)
        )
    blocks = s["blocks"]
    fresh = []
    lane_of = (iota((128, JOINT), 1) & 15) == iota((128, JOINT), 0)
    group_of = (iota((32, JOINT), 1) >> 4) == iota((32, JOINT), 0)
    for step in range(2):
        for k in range(3):
            blocks[pl.ds(step * 96 + k, 32, stride=3), :] = queries[pl.ds(step * 4 + k, 32, stride=8), :]
        keyval = queries[pl.ds(step * 4 + 3, 32, stride=8), :].astype(BF16)
        copies = jnp.dot(keyval, jnp.where(lane_of, 1.0, 0.0).astype(BF16), preferred_element_type=F32)
        fresh.append(jnp.sum(jnp.where(group_of, copies, 0.0), axis=0, keepdims=True))
    rows128 = iota((128, JOINT), 0)
    fresh_all = jnp.where(rows128 == 0, fresh[0], jnp.where(rows128 == 1, fresh[1], 0.0)).astype(BF16)
    query = jnp.concatenate(
        [
            jnp.concatenate(
                [blocks[pl.ds(step * 96 + half, 48, stride=2), :] for half in (0, 1)], axis=1
            )
            for step in range(2)
        ],
        axis=0,
    ).astype(BF16)
    inv_root = HEAD_DIM ** (-0.5)
    over_keys = (((1,), (1,)), ((), ()))
    loads[3].wait()
    cached = lax.dot_general(query, s["keys"][...], over_keys, preferred_element_type=F32) * inv_root
    cached = jnp.where(iota((96, CACHE), 1) < lengths[0], cached, MASKED_SCORE)
    new = lax.dot_general(query, fresh_all[:, :HEAD_DIM], over_keys, preferred_element_type=F32) * inv_root
    lane, row = iota((96, 128), 1), iota((96, 128), 0)
    new = jnp.where((lane == 0) | ((lane == 1) & (row >= HEADS)), new, MASKED_SCORE)
    peak = jnp.maximum(jnp.max(cached, axis=1, keepdims=True), jnp.max(new, axis=1, keepdims=True))
    cached = jnp.exp(cached - peak)
    new = jnp.exp(new - peak)
    total = jnp.sum(cached, axis=1, keepdims=True) + jnp.sum(new, axis=1, keepdims=True)
    loads[4].wait()
    weighted = jnp.dot(cached.astype(BF16), s["values"][...], preferred_element_type=F32) + jnp.dot(
        new.astype(BF16), fresh_all[:, HEAD_DIM:], preferred_element_type=F32
    )
    attended = (weighted / total).astype(BF16).astype(F32)

    att_blocks, leaving, landed = s["att_blocks"], s["leaving"], s["landed"]
    for step in range(2):
        for half in (0, 1):
            att_blocks[pl.ds(step * 96 + half, 48, stride=2), :] = attended[
                step * 48 : (step + 1) * 48, half * 128 : (half + 1) * 128
            ]
        for k in range(3):
            leaving[pl.ds(step * 4 + k, 32, stride=8), :] = att_blocks[pl.ds(step * 96 + k, 32, stride=3), :]
        leaving[pl.ds(step * 4 + 3, 32, stride=8), :] = jnp.zeros((32, 128), F32)
    for ry, rx in hidden_peers:
        slot = POS[(-ry) % Y] * X + (-rx) % X
        links.push(
            leaving.at[pl.ds(pl.multiple_of(links.hidden(ry, rx) * 8, 8), 8)],
            landed.at[pl.ds(slot * 8, 8)],
            dict(ry=ry, rx=rx),
            ("landed", slot),
        )
    landed[0:8] = leaving[pl.ds(pl.multiple_of(h * 8, 8), 8)]

    along_f32, along, whole, whole_f32 = s["along_f32"], s["along"], s["whole"], s["whole_f32"]
    feature_rows, product = s["feature_rows"], s["product"]

    def pass_along(chunk):
        p0, p1 = CHUNKS[chunk]
        count = p1 - p0
        span = slice(p0 * 16, p1 * 16)
        part = pl.ds(p0 * 16, count * 16)
        for slot in range(max(p0 * X, 1), p1 * X):
            links.arrive(landed.at[pl.ds(slot * 8, 8)], ("landed", slot))
        for step in range(2):
            for k in range(4):
                along_f32[step, pl.ds(p0 * 16 + k, count * 4, stride=4), :] = landed[
                    pl.ds(p0 * 32 + step * 4 + k, count * 4, stride=8), :
                ]
            along[step, span] = along_f32[step, span].astype(BF16)
        for rz, rc in width_peers:
            links.push(
                along.at[links.core(rc), part],
                whole.at[w, part],
                dict(rz=rz, rc=rc),
                ("whole", chunk, (-rz) % Z, rc),
            )
        whole[w, span] = along[c, span]

    def multiply(chunk):
        p0, p1 = CHUNKS[chunk]
        count = p1 - p0
        span = slice(p0 * 16, p1 * 16)
        for rz, rc in width_peers:
            links.arrive(whole.at[links.width(rz, rc), pl.ds(p0 * 16, count * 16)], ("whole", chunk, rz, rc))
        for row in range(16):
            whole_f32[row, span] = whole[row, span].astype(F32)
            for k in range(3):
                feature_rows[k, pl.ds(p0 * 64 + row, count * 4, stride=16), :] = whole_f32[
                    row, pl.ds(p0 * 16 + k, count * 4, stride=4), :
                ]
        if chunk == 3:
            links.arrive(out_w.at[1 - c], "out_w")
        operand = jnp.concatenate([feature_rows[k, p0 * 64 : p1 * 64] for k in range(3)], axis=1).astype(BF16)
        for half in (0, 1):
            product[p0 * 64 : p1 * 64, half * WIDTH_DEV : (half + 1) * WIDTH_DEV] = jnp.dot(
                operand, out_w[half], preferred_element_type=F32
            )

    sa, sb, la, lax_, lbx, lby = s["sa"], s["sb"], s["la"], s["lax"], s["lbx"], s["lby"]

    def own_a(ry, rx):
        at = (POS[ry] * X + rx) * 16
        return product[at : at + 16, 0:CUT]

    def own_b(ry, rx):
        at = (POS[ry] * X + rx) * 16
        return product[at : at + 16, CUT:WIDTH_CHIP]

    def y_slot(ry, up):
        return 8 if ry == 0 and not up else POS[ry]

    def from_y(buffer, name, ry, rx, up):
        slot = buffer.at[y_slot(ry, up), rx]
        links.arrive(slot, (name, ry, rx, up))
        return slot[...].astype(F32)

    def to_y(name, source, buffer, ry, rx, up):
        to = ry - 1 if up else (ry + 1) % Y
        links.push(source, buffer.at[y_slot(to, up), rx], dict(ry=1 if up else -1), (name, to, rx, up))

    def a_sums(distance):
        for ry in BY_DISTANCE[distance]:
            for rx in range(X):
                if ry == 4:
                    up = rx < 2
                else:
                    up = ry <= 3
                total = own_a(ry, rx)
                if distance in (1, 2) or (distance == 3 and up == (rx < 2)):
                    total = total + from_y(la, "la", ry, rx, up)
                sa[POS[ry], rx] = total.astype(BF16)
                to_y("la", sa.at[POS[ry], rx], la, ry, rx, up)

    def a_rows():
        for rx in (2, 1, 3):
            total = own_a(0, rx) + from_y(la, "la", 0, rx, True) + from_y(la, "la", 0, rx, False)
            sa[0, rx] = total.astype(BF16)
            links.push(sa.at[0, rx], lax_.at[rx - 1], dict(rx=rx), ("lax", rx))

    def from_x(ry, slot):
        links.arrive(lbx.at[POS[ry], slot], ("lbx", ry, slot))
        return lbx[POS[ry], slot].astype(F32)

    def to_x(ry, rx, slot, right):
        links.push(sb.at[POS[ry], rx], lbx.at[POS[ry], slot], dict(rx=1 if right else -1), ("lbx", ry, slot))

    def b_far(distance):
        for ry in BY_DISTANCE[distance]:
            right = POS[ry] % 2 == 0
            sb[POS[ry], 2] = own_b(ry, 2).astype(BF16)
            to_x(ry, 2, 1 if right else 3, right)

    def b_near(distance):
        for ry in BY_DISTANCE[distance]:
            for rx in (1, 3):
                total = own_b(ry, rx)
                if (rx == 1) == (POS[ry] % 2 == 0):
                    total = total + from_x(ry, rx)
                sb[POS[ry], rx] = total.astype(BF16)
                to_x(ry, rx, 0 if rx == 1 else 2, rx == 1)

    def b_column(ry):
        return own_b(ry, 0) + from_x(ry, 0) + from_x(ry, 2)

    def b_sums(distance):
        for ry in BY_DISTANCE[distance]:
            up = ry <= 4
            total = b_column(ry)
            if distance in (1, 2) or ry == 3:
                total = total + from_y(lby, "lby", ry, 0, up)
            sb[POS[ry], 0] = total.astype(BF16)
            to_y("lby", sb.at[POS[ry], 0], lby, ry, 0, up)

    for chunk in (3, 2, 1, 0):
        pass_along(chunk)
    for turn in range(7):
        if turn < 4:
            multiply(3 - turn)
        distance = 4 - turn
        if distance >= 1:
            a_sums(distance)
        if distance == 0:
            a_rows()
        if distance >= 0:
            b_far(distance)
        if 0 <= distance + 1 <= 4:
            b_near(distance + 1)
        if 1 <= distance + 2 <= 4:
            b_sums(distance + 2)
    last_a = own_a(0, 0) + from_y(la, "la", 0, 0, True) + from_y(la, "la", 0, 0, False)
    for rx in (1, 3, 2):
        links.arrive(lax_.at[rx - 1], ("lax", rx))
        last_a = last_a + lax_[rx - 1].astype(F32)
    last_b = b_column(0) + from_y(lby, "lby", 0, 0, True) + from_y(lby, "lby", 0, 0, False)
    done = jnp.concatenate([last_a, last_b], axis=1).astype(BF16)
    result, swapped = s["result"], s["swapped"]
    for half in (0, 1):
        result[half] = done[:, half * WIDTH_DEV : (half + 1) * WIDTH_DEV]
    links.push(result.at[1 - c], swapped.at[c], dict(rc=1), "swapped")
    out[c] = result[c]
    links.arrive(swapped.at[1 - c], "swapped")
    out[1 - c] = swapped[1 - c]
    links.finish()
    assert len(links.sent) <= SENDS and len(links.keys) <= ARRIVALS


SCRATCH = dict(
    stats=((16, 8, 128), F32),
    gains=((2, 8, WIDTH_DEV), F32),
    halves=((2, 16, WIDTH_DEV), BF16),
    joint=((WIDTH_CHIP, JOINT), BF16),
    keyval_w=((WIDTH_DEV, 16), BF16),
    out_w=((2, FEAT_DEV, WIDTH_DEV), BF16),
    keys=((CACHE, HEAD_DIM), BF16),
    values=((CACHE, HEAD_DIM), BF16),
    ga=((Y, X, 16, CUT), BF16),
    gb=((Y, X, 16, REST), BF16),
    acc=((4, 512, 128), F32),
    spread_out=((16, 128, 128), F32),
    packed=((16, 128, 128), BF16),
    shares=((2, Z, 128, 128), BF16),
    owned_sum=((2, 128, 128), F32),
    owned=((256, 128), F32),
    queries=((256, 128), F32),
    blocks=((192, 128), F32),
    att_blocks=((192, 128), F32),
    leaving=((256, 128), F32),
    landed=((256, 128), F32),
    along_f32=((2, 128, 128), F32),
    along=((2, 128, 128), BF16),
    whole=((16, 128, 128), BF16),
    whole_f32=((16, 128, 128), F32),
    feature_rows=((3, 512, 128), F32),
    product=((512, WIDTH_CHIP), F32),
    sa=((Y, X, 16, CUT), BF16),
    sb=((Y, X, 16, REST), BF16),
    la=((Y + 1, X, 16, CUT), BF16),
    lax=((3, 16, CUT), BF16),
    lbx=((Y, X, 16, REST), BF16),
    lby=((Y + 1, 1, 16, REST), BF16),
    result=((2, 16, WIDTH_DEV), BF16),
    swapped=((2, 16, WIDTH_DEV), BF16),
)


def shards(tokens, gain, query_weight, keyval_weight, out_weight, key_cache, value_cache, lengths):
    names = list(SCRATCH)

    def body(*refs):
        scratch = dict(zip(names, refs[9:]))
        scratch.update(send_sems=refs[-3], recv_sems=refs[-2], local_sems=refs[-1])
        kernel(*refs[:9], scratch)

    vmem, smem, hbm = (pl.BlockSpec(memory_space=space) for space in (pltpu.VMEM, pltpu.SMEM, pl.ANY))
    return pl.pallas_call(
        body,
        out_shape=jax.ShapeDtypeStruct(tokens.shape, BF16),
        in_specs=[vmem, vmem, smem, hbm, hbm, hbm, hbm, hbm],
        out_specs=vmem,
        scratch_shapes=[pltpu.VMEM(shape, dtype) for shape, dtype in SCRATCH.values()]
        + [
            pltpu.SemaphoreType.DMA((SENDS,)),
            pltpu.SemaphoreType.DMA((ARRIVALS,)),
            pltpu.SemaphoreType.DMA((5,)),
        ],
        compiler_params=pltpu.CompilerParams(
            collective_id=0, has_side_effects=True, vmem_limit_bytes=48 * 1024 * 1024
        ),
    )(tokens, gain.reshape(1, -1), lengths, query_weight, keyval_weight, out_weight, key_cache, value_cache)


def solution(mesh):
    return jax.shard_map(
        shards,
        mesh=mesh,
        in_specs=(
            P(None, "hidden", "width"),
            P("width"),
            P("width", "hidden"),
            P("width", "hidden"),
            P("hidden", "width"),
            P(("hidden", "width"), None, None),
            P(("hidden", "width"), None, None),
            P(("hidden", "width")),
        ),
        out_specs=P(None, "hidden", "width"),
        check_vma=False,
    )
```

```python
import jax
import jax.numpy as jnp
from jax import lax
from jax.experimental import pallas as pl
from jax.experimental.pallas import tpu as pltpu
from jax.sharding import PartitionSpec as P

MESH = pl.DeviceIdType.MESH
F32, BF16 = jnp.float32, jnp.bfloat16

D = 18432
HEADS = 48
HEAD_DIM = 256
CACHE = 2048
FEAT_DEV = 384
WIDTH_DEV = 1152
WIDTH_CHIP = 2304
JOINT = 512
EPS = 1e-05
MASKED_SCORE = -1e30

X, Y, Z = 4, 8, 8
CUT = 1024
REST = WIDTH_CHIP - CUT
ORDER = (0, 1, 7, 2, 6, 3, 5, 4)
POS = {ry: pos for pos, ry in enumerate(ORDER)}
CHUNKS = ((0, 3), (3, 5), (5, 7), (7, 8))
HALVES = ((0, 4), (4, 8))
STAT = 16

VMEM_BYTES = 60 * 1024 * 1024
ARRIVALS = 144
ARRIVAL_ORDER = (
    ("b", 7, 0), ("b", 1, 0), ("b", 0, 3), ("b", 0, 1), ("a", 0, 3), ("a", 0, 1),
    ("b", 6, 0), ("b", 2, 0), ("a", 7, 0), ("a", 1, 0), ("a", 0, 2), ("b", 7, 3),
    ("b", 7, 1), ("a", 7, 3), ("a", 1, 3), ("b", 1, 3), ("b", 1, 1), ("a", 7, 1),
    ("a", 1, 1), ("b", 0, 2), ("b", 5, 0), ("b", 6, 1), ("b", 3, 0), ("b", 6, 3),
    ("a", 6, 0), ("a", 2, 0), ("b", 2, 1), ("b", 2, 3), ("a", 7, 2), ("a", 1, 2),
    ("a", 6, 3), ("a", 2, 3), ("b", 1, 2), ("b", 7, 2), ("a", 6, 1), ("a", 2, 1),
    ("b", 4, 0), ("b", 5, 3), ("b", 5, 1), ("a", 3, 0), ("a", 5, 0), ("b", 3, 3),
    ("b", 3, 1), ("a", 2, 2), ("a", 6, 2), ("a", 3, 3), ("b", 6, 2), ("b", 2, 2),
    ("a", 5, 3), ("a", 3, 1), ("a", 5, 1), ("b", 4, 3), ("b", 4, 1), ("a", 4, 0),
    ("a", 3, 2), ("b", 3, 2), ("a", 5, 2), ("a", 4, 3), ("a", 4, 1), ("b", 4, 2),
    ("b", 5, 2), ("a", 4, 2),
)


def forwards(part, ry, rx):
    if part == "a":
        along = [(1, 0), (-1, 0)] if ry == 0 else []
        if ry >= 6 or (ry == 5 and rx < 2):
            along = [(1, 0)]
        if ry in (1, 2) or (ry == 3 and rx >= 2):
            along = [(-1, 0)]
        return along + ([(0, 1), (0, -1), (0, 2)] if (ry, rx) == (0, 0) else [])
    if rx == 0:
        along = {0: [(1, 0), (-1, 0), (2, 0), (-2, 0)], 6: [(1, 0)], 5: [(1, 0)], 2: [(-1, 0)]}.get(ry, [])
        return along + [(0, 1), (0, -1)] + ([(0, 2)] if ry == 4 else [])
    if ry != 4 and rx == (3 if POS[ry] % 2 == 0 else 1):
        return [(0, 1 if rx == 3 else -1)]
    return []


def reached(part, ry, rx):
    return [(dy, dx, (part, (ry - dy) % Y, (rx - dx) % X)) for dy, dx in forwards(part, ry, rx)]


BEFORE = {
    key: (-dy, -dx)
    for part in "ab"
    for ry in range(Y)
    for rx in range(X)
    for dy, dx, key in reached(part, ry, rx)
}


class Links:
    def __init__(self, send_sem, recv_sems):
        self.send_sem = send_sem
        self.recv_sems = recv_sems
        self.sent = []
        self.keys = {}
        self.devices = {}
        self.h = lax.axis_index("hidden")
        self.w = lax.axis_index("width")
        self.y, self.x = lax.div(self.h, X), lax.rem(self.h, X)
        self.z, self.c = lax.div(self.w, 2), lax.rem(self.w, 2)

    def hidden(self, ry, rx):
        return lax.rem(self.y + ry % Y, Y) * X + lax.rem(self.x + rx % X, X)

    def width(self, rz, rc):
        return lax.rem(self.z + rz % Z, Z) * 2 + self.core(rc)

    def core(self, rc):
        return self.c if rc == 0 else 1 - self.c

    def device(self, ry=0, rx=0, rz=0, rc=0):
        at = (ry % Y, rx % X, rz % Z, rc)
        if at not in self.devices:
            self.devices[at] = {"hidden": self.hidden(*at[:2]), "width": self.width(*at[2:])}
        return self.devices[at]

    def arrival(self, key):
        return self.recv_sems.at[self.keys.setdefault(key, len(self.keys))]

    def push(self, src, dst, to, key):
        copy = pltpu.make_async_remote_copy(
            src_ref=src,
            dst_ref=dst,
            send_sem=self.send_sem.at[0],
            recv_sem=self.arrival(key),
            device_id=self.device(**to),
            device_id_type=MESH,
        )
        copy.start()
        self.sent.append(copy)

    def arrive(self, dst, key):
        pltpu.make_async_remote_copy(
            src_ref=dst,
            dst_ref=dst,
            send_sem=self.send_sem.at[0],
            recv_sem=self.arrival(key),
            device_id=self.device(rc=1),
            device_id_type=MESH,
        ).wait_recv()

    def finish(self):
        for copy in self.sent:
            copy.wait_send()


def iota(shape, axis):
    return lax.broadcasted_iota(jnp.int32, shape, axis)


def pieces(values):
    high = values.astype(BF16)
    rest = values - high.astype(F32)
    middle = rest.astype(BF16)
    return high, middle, (rest - middle.astype(F32)).astype(BF16)


def sum_all(terms):
    total = terms[0]
    for term in terms[1:]:
        total = total + term
    return total


def kernel(tokens, gain, lengths, query_weight, keyval_weight, out_weight, key_cache, value_cache, out, s):
    links = Links(s["send_sem"], s["recv_sems"])
    c, h, w = links.c, links.h, links.w
    width_peers = [(rz, rc) for rz in (4, 3, 5, 2, 6, 1, 7, 0) for rc in (0, 1) if (rz, rc) != (0, 0)]
    hidden_peers = [(ry, rx) for ry in reversed(ORDER) for rx in (2, 1, 3, 0) if (ry, rx) != (0, 0)]

    barrier = pltpu.get_barrier_semaphore()
    for rz, rc in width_peers:
        pl.semaphore_signal(barrier, inc=1, device_id=links.device(rz=rz, rc=rc), device_id_type=MESH)
    for ry, rx in hidden_peers:
        pl.semaphore_signal(barrier, inc=1, device_id=links.device(ry=ry, rx=rx), device_id_type=MESH)

    joint, out_w = s["joint"], s["out_w"]
    mine = pl.ds(pl.multiple_of(c * WIDTH_DEV, WIDTH_DEV), WIDTH_DEV)
    others = pl.ds(pl.multiple_of((1 - c) * WIDTH_DEV, WIDTH_DEV), WIDTH_DEV)
    local = s["local_sems"]
    loads = [
        pltpu.make_async_copy(keyval_weight, s["keyval_w"], local.at[0]),
        pltpu.make_async_copy(query_weight, joint.at[mine, pl.ds(0, FEAT_DEV)], local.at[1]),
        pltpu.make_async_copy(out_weight, out_w.at[c], local.at[2]),
        pltpu.make_async_copy(key_cache.at[0], s["keys"], local.at[3]),
        pltpu.make_async_copy(value_cache.at[0], s["values"], local.at[4]),
    ]
    for load in loads:
        load.start()

    gain_row = gain[...][None]
    rows = tokens[...].astype(F32).reshape(32, WIDTH_DEV)
    own_mean = jnp.sum(rows, axis=1, keepdims=True) * (1.0 / WIDTH_DEV)
    centered = rows - own_mean
    own_spread = jnp.sum(centered * centered, axis=1, keepdims=True)
    lane = iota((32, 128), 1) - (STAT + 8 * c)
    lanes = jnp.zeros((32, 128), F32)
    for at, piece in enumerate(pieces(own_mean) + pieces(own_spread)):
        lanes = jnp.where(lane == at, piece.astype(F32), lanes)
    own_rows, both = s["own_rows"], s["both"]
    own_rows[...] = jnp.concatenate([centered * gain_row, lanes], axis=1).astype(BF16).reshape(2, 16, WIDTH_DEV + 128)
    both[c] = own_rows[c]

    pl.semaphore_wait(barrier, len(width_peers) + len(hidden_peers))
    links.push(own_rows.at[1 - c], both.at[c], dict(rc=1), "both")

    ga, gb = s["ga"], s["gb"]
    block = {"a": ga, "b": gb}

    def pass_on(part, ry, rx):
        for dy, dx, key in reached(part, ry, rx):
            links.push(
                block[part].at[POS[ry], rx], block[part].at[POS[key[1]], key[2]], dict(ry=dy, rx=dx), key
            )

    links.arrive(both.at[1 - c], "both")
    ga[0, 0] = both[0, :, :CUT]
    gb[0, 0] = jnp.concatenate(
        [both[0, :, CUT:WIDTH_DEV], both[1, :, :WIDTH_DEV], both[0, :, WIDTH_DEV:] + both[1, :, WIDTH_DEV:]], axis=1
    )
    pass_on("b", 0, 0)
    pass_on("a", 0, 0)

    loads[0].wait()
    across = jnp.concatenate([s["keyval_w"][...].astype(F32), jnp.zeros((112, WIDTH_DEV), F32)], axis=0)
    joint[mine, FEAT_DEV:JOINT] = across.T.astype(BF16)
    loads[1].wait()
    links.push(joint.at[mine], joint.at[mine], dict(rc=1), "joint")
    eighth = iota((8, WIDTH_DEV), 0)
    gain_rows = jnp.zeros((8, WIDTH_DEV), F32)
    for at, piece in enumerate(pieces(gain_row)):
        gain_rows = jnp.where(eighth == at, piece.astype(F32), gain_rows)
    weight_sum = jnp.sum(
        jnp.dot(gain_rows.astype(BF16), joint[mine, :], preferred_element_type=F32), axis=0, keepdims=True
    )
    weight_sums = s["weight_sums"]
    eighth = iota((8, 128), 0)
    weight_tile = jnp.zeros((8, 128), F32)
    for k in range(4):
        weight_tile = jnp.where(eighth == k, weight_sum[:, k * 128 : (k + 1) * 128], weight_tile)
    weight_sums[c] = weight_tile
    for rz, rc in width_peers:
        links.push(weight_sums.at[c], weight_sums.at[((-rz) % Z) * 2 + c], dict(rz=rz, rc=rc), "weight_sums")
    loads[2].wait()
    links.push(out_w.at[c], out_w.at[c], dict(rc=1), "out_w")

    acc, spread_out, packed, shares = s["acc"], s["spread_out"], s["packed"], s["shares"]
    each, total, owned, queries = s["each"], s["total"], s["owned"], s["queries"]

    def project(chunk):
        p0, p1 = CHUNKS[chunk]
        count = p1 - p0
        if chunk == 0:
            links.arrive(joint.at[others], "joint")
        stretch = gb[p0:p1].reshape(count * 64, REST + 128)
        partial = jnp.dot(
            ga[p0:p1].reshape(count * 64, CUT), joint[0:CUT], preferred_element_type=F32
        ) + jnp.dot(stretch[:, :REST], joint[CUT:WIDTH_CHIP], preferred_element_type=F32)
        for k in range(4):
            columns = partial[:, k * 128 : (k + 1) * 128]
            acc[k, p0 * 64 : p1 * 64] = columns if k < 3 else columns + stretch[:, REST:].astype(F32)
        span = slice(p0 * 16, p1 * 16)
        for row in range(16):
            for k in range(4):
                spread_out[row, pl.ds(p0 * 16 + k, count * 4, stride=4), :] = acc[
                    k, pl.ds(p0 * 64 + row, count * 4, stride=16), :
                ]
            packed[row, span] = spread_out[row, span].astype(BF16)
        part = pl.ds(p0 * 16, count * 16)
        for rz, rc in width_peers:
            links.push(
                packed.at[links.width(rz, rc), part],
                shares.at[c * Z + (-rz) % Z, part],
                dict(rz=rz, rc=rc),
                ("shares", chunk),
            )
        shares[c * Z, span] = packed[w, span]

    def hand_out(chunk):
        p0, p1 = CHUNKS[chunk]
        count = (p1 - p0) * 4
        span = slice(p0 * 16, p1 * 16)
        links.arrive(shares.at[pl.ds(0, 15), pl.ds(p0 * 16, (p1 - p0) * 16)], ("shares", chunk))
        if chunk == 0:
            links.arrive(weight_sums.at[pl.ds(0, 15)], "weight_sums")
        lane = iota((count, 128), 1) - STAT

        def picked(values, chosen):
            return jnp.sum(jnp.where(chosen, values, 0.0), axis=1, keepdims=True)

        for step in range(2):
            terms = [shares[step * Z + rz, span].astype(F32) for rz in range(Z)]
            for rz in range(Z):
                each[rz, span] = terms[rz]
            total[span] = sum_all(terms)
            means = []
            for rz in range(Z):
                stats = each[rz, pl.ds(p0 * 16 + 3, count, stride=4), :]
                means += [picked(stats, (lane >= first) & (lane < first + 3)) for first in (0, 8)]
            spread = picked(
                total[pl.ds(p0 * 16 + 3, count, stride=4), :],
                ((lane >= 3) & (lane < 6)) | ((lane >= 11) & (lane < 14)),
            )
            mean = sum_all(means) * (1.0 / 16)
            apart = [own - mean for own in means]
            spread = spread + WIDTH_DEV * sum_all([gap * gap for gap in apart])
            scale = lax.rsqrt(spread * (1.0 / D) + EPS)
            for k in range(4):
                values = total[pl.ds(p0 * 16 + k, count, stride=4), :]
                for at, gap in enumerate(apart):
                    values = values + gap * weight_sums[at, k : k + 1, :]
                owned[pl.ds(p0 * 32 + step * 4 + k, count, stride=8), :] = values * scale
        here_h = pl.ds(pl.multiple_of(h * 8, 8), 8)
        for pos in range(p0, p1):
            ry = ORDER[pos]
            for rx in range(X):
                tile = pl.ds((pos * X + rx) * 8, 8)
                if (ry, rx) == (0, 0):
                    queries[here_h] = owned[tile]
                else:
                    links.push(owned.at[tile], queries.at[here_h], dict(ry=ry, rx=rx), "queries")

    missing = [{key for key in ARRIVAL_ORDER if p0 <= POS[key[1]] < p1} for p0, p1 in CHUNKS]
    waiting = []
    for key in ARRIVAL_ORDER:
        part, ry, rx = key
        links.arrive(block[part].at[POS[ry], rx], key)
        pass_on(*key)
        for chunk in range(len(CHUNKS)):
            if key in missing[chunk]:
                missing[chunk].discard(key)
                if not missing[chunk]:
                    project(chunk)
                    if waiting:
                        hand_out(waiting.pop(0))
                    waiting.append(chunk)
    for chunk in waiting:
        hand_out(chunk)

    links.arrive(queries.at[pl.ds(0, 31 * 8)], "queries")
    blocks = s["blocks"]
    fresh = []
    lane_of = (iota((128, JOINT), 1) & 15) == iota((128, JOINT), 0)
    group_of = (iota((32, JOINT), 1) >> 4) == iota((32, JOINT), 0)
    for step in range(2):
        for k in range(3):
            blocks[pl.ds(step * 96 + k, 32, stride=3), :] = queries[pl.ds(step * 4 + k, 32, stride=8), :]
        keyval = queries[pl.ds(step * 4 + 3, 32, stride=8), :].astype(BF16)
        copies = jnp.dot(keyval, jnp.where(lane_of, 1.0, 0.0).astype(BF16), preferred_element_type=F32)
        fresh.append(jnp.sum(jnp.where(group_of, copies, 0.0), axis=0, keepdims=True))
    rows128 = iota((128, JOINT), 0)
    fresh_all = jnp.where(rows128 == 0, fresh[0], jnp.where(rows128 == 1, fresh[1], 0.0)).astype(BF16)
    query = jnp.concatenate(
        [
            jnp.concatenate(
                [blocks[pl.ds(step * 96 + half, 48, stride=2), :] for half in (0, 1)], axis=1
            )
            for step in range(2)
        ],
        axis=0,
    ).astype(BF16)
    inv_root = HEAD_DIM ** (-0.5)
    over_keys = (((1,), (1,)), ((), ()))
    loads[3].wait()
    cached = lax.dot_general(query, s["keys"][...], over_keys, preferred_element_type=F32) * inv_root
    cached = jnp.where(iota((96, CACHE), 1) < lengths[0], cached, MASKED_SCORE)
    new = lax.dot_general(query, fresh_all[:, :HEAD_DIM], over_keys, preferred_element_type=F32) * inv_root
    lane, row = iota((96, 128), 1), iota((96, 128), 0)
    new = jnp.where((lane == 0) | ((lane == 1) & (row >= HEADS)), new, MASKED_SCORE)
    peak = jnp.maximum(jnp.max(cached, axis=1, keepdims=True), jnp.max(new, axis=1, keepdims=True))
    cached = jnp.exp(cached - peak)
    new = jnp.exp(new - peak)
    total = jnp.sum(cached, axis=1, keepdims=True) + jnp.sum(new, axis=1, keepdims=True)
    loads[4].wait()
    weighted = jnp.dot(cached.astype(BF16), s["values"][...], preferred_element_type=F32) + jnp.dot(
        new.astype(BF16), fresh_all[:, HEAD_DIM:], preferred_element_type=F32
    )
    attended = (weighted / total).astype(BF16).astype(F32)

    att_blocks, leaving, landed = s["att_blocks"], s["leaving"], s["landed"]
    for step in range(2):
        for half in (0, 1):
            att_blocks[pl.ds(step * 96 + half, 48, stride=2), :] = attended[
                step * 48 : (step + 1) * 48, half * 128 : (half + 1) * 128
            ]
        for k in range(3):
            leaving[pl.ds(step * 4 + k, 32, stride=8), :] = att_blocks[pl.ds(step * 96 + k, 32, stride=3), :]
        leaving[pl.ds(step * 4 + 3, 32, stride=8), :] = jnp.zeros((32, 128), F32)
    for ry, rx in hidden_peers:
        slot = POS[(-ry) % Y] * X + (-rx) % X
        links.push(
            leaving.at[pl.ds(pl.multiple_of(links.hidden(ry, rx) * 8, 8), 8)],
            landed.at[pl.ds(slot * 8, 8)],
            dict(ry=ry, rx=rx),
            ("landed", slot < 16),
        )
    landed[0:8] = leaving[pl.ds(pl.multiple_of(h * 8, 8), 8)]

    along_f32, along, whole, whole_f32 = s["along_f32"], s["along"], s["whole"], s["whole_f32"]
    feature_rows, product = s["feature_rows"], s["product"]

    def pass_along(half):
        p0, p1 = HALVES[half]
        span = slice(p0 * 12, p1 * 12)
        part = pl.ds(p0 * 12, 48)
        links.arrive(landed.at[pl.ds(p0 * 32, (16 if half else 15) * 8)], ("landed", half == 0))
        for step in range(2):
            for k in range(3):
                along_f32[step, pl.ds(p0 * 12 + k, 16, stride=3), :] = landed[
                    pl.ds(p0 * 32 + step * 4 + k, 16, stride=8), :
                ]
            along[step, span] = along_f32[step, span].astype(BF16)
        for rz, rc in width_peers:
            links.push(along.at[links.core(rc), part], whole.at[w, part], dict(rz=rz, rc=rc), ("whole", half))
        whole[w, span] = along[c, span]

    def multiply(half):
        p0, p1 = HALVES[half]
        span = slice(p0 * 12, p1 * 12)
        links.arrive(whole.at[pl.ds(0, 15), pl.ds(p0 * 12, 48)], ("whole", half))
        for row in range(16):
            whole_f32[row, span] = whole[row, span].astype(F32)
            for k in range(3):
                feature_rows[k, pl.ds(p0 * 64 + row, 16, stride=16), :] = whole_f32[
                    row, pl.ds(p0 * 12 + k, 16, stride=3), :
                ]
        operand = jnp.concatenate([feature_rows[k, p0 * 64 : p1 * 64] for k in range(3)], axis=1).astype(BF16)
        if half:
            links.arrive(out_w.at[1 - c], "out_w")
        for side in (0, 1):
            product[p0 * 64 : p1 * 64, side * WIDTH_DEV : (side + 1) * WIDTH_DEV] = jnp.dot(
                operand, out_w[side], preferred_element_type=F32
            )

    pass_along(1)
    pass_along(0)

    staged = {"a": s["sa"], "b": s["sb"]}
    landing = {"a": s["la"], "b": s["lb"]}
    columns = {"a": slice(0, CUT), "b": slice(CUT, WIDTH_CHIP)}
    multiplied = set()

    def summed(part, ry, rx):
        half = 1 if POS[ry] >= 4 else 0
        if half not in multiplied:
            multiplied.add(half)
            multiply(half)
        at = (POS[ry] * X + rx) * 16
        terms = [product[at : at + 16, columns[part]]]
        for _, _, key in reached(part, ry, rx):
            slot = landing[part].at[POS[key[1]], key[2]]
            links.arrive(slot, ("sum",) + key)
            terms.append(slot[...].astype(F32))
        return sum_all(terms)

    multiplied.add(1)
    multiply(1)
    for key in reversed(ARRIVAL_ORDER):
        part, ry, rx = key
        at = (POS[ry], rx)
        staged[part][at] = summed(*key).astype(BF16)
        dy, dx = BEFORE[key]
        links.push(staged[part].at[at], landing[part].at[at], dict(ry=dy, rx=dx), ("sum",) + key)
    done = jnp.concatenate([summed("a", 0, 0), summed("b", 0, 0)], axis=1).astype(BF16)
    result, swapped = s["result"], s["swapped"]
    for side in (0, 1):
        result[side] = done[:, side * WIDTH_DEV : (side + 1) * WIDTH_DEV]
    links.push(result.at[1 - c], swapped.at[c], dict(rc=1), "swapped")
    out[c] = result[c]
    links.arrive(swapped.at[1 - c], "swapped")
    out[1 - c] = swapped[1 - c]
    links.finish()
    assert len(links.keys) <= ARRIVALS


SCRATCH = dict(
    own_rows=((2, 16, WIDTH_DEV + 128), BF16),
    both=((2, 16, WIDTH_DEV + 128), BF16),
    weight_sums=((16, 8, 128), F32),
    joint=((WIDTH_CHIP, JOINT), BF16),
    keyval_w=((16, WIDTH_DEV), BF16),
    out_w=((2, FEAT_DEV, WIDTH_DEV), BF16),
    keys=((CACHE, HEAD_DIM), BF16),
    values=((CACHE, HEAD_DIM), BF16),
    ga=((Y, X, 16, CUT), BF16),
    gb=((Y, X, 16, REST + 128), BF16),
    acc=((4, 512, 128), F32),
    spread_out=((16, 128, 128), F32),
    packed=((16, 128, 128), BF16),
    shares=((16, 128, 128), BF16),
    each=((Z, 128, 128), F32),
    total=((128, 128), F32),
    owned=((256, 128), F32),
    queries=((256, 128), F32),
    blocks=((192, 128), F32),
    att_blocks=((192, 128), F32),
    leaving=((256, 128), F32),
    landed=((256, 128), F32),
    along_f32=((2, 96, 128), F32),
    along=((2, 96, 128), BF16),
    whole=((16, 96, 128), BF16),
    whole_f32=((16, 96, 128), F32),
    feature_rows=((3, 512, 128), F32),
    product=((512, WIDTH_CHIP), F32),
    sa=((Y, X, 16, CUT), BF16),
    sb=((Y, X, 16, REST), BF16),
    la=((Y, X, 16, CUT), BF16),
    lb=((Y, X, 16, REST), BF16),
    result=((2, 16, WIDTH_DEV), BF16),
    swapped=((2, 16, WIDTH_DEV), BF16),
)


def shards(tokens, gain, query_weight, keyval_weight, out_weight, key_cache, value_cache, lengths):
    names = list(SCRATCH)

    def body(*refs):
        scratch = dict(zip(names, refs[9:]))
        scratch.update(send_sem=refs[-3], recv_sems=refs[-2], local_sems=refs[-1])
        kernel(*refs[:9], scratch)

    vmem, smem, hbm = (pl.BlockSpec(memory_space=space) for space in (pltpu.VMEM, pltpu.SMEM, pl.ANY))
    return pl.pallas_call(
        body,
        out_shape=jax.ShapeDtypeStruct(tokens.shape, BF16),
        in_specs=[vmem, vmem, smem, hbm, hbm, hbm, hbm, hbm],
        out_specs=vmem,
        scratch_shapes=[pltpu.VMEM(shape, dtype) for shape, dtype in SCRATCH.values()]
        + [
            pltpu.SemaphoreType.DMA((1,)),
            pltpu.SemaphoreType.DMA((ARRIVALS,)),
            pltpu.SemaphoreType.DMA((5,)),
        ],
        compiler_params=pltpu.CompilerParams(
            collective_id=0, has_side_effects=True, vmem_limit_bytes=VMEM_BYTES
        ),
    )(tokens, gain, lengths, query_weight, keyval_weight.T, out_weight, key_cache, value_cache)


def solution(mesh):
    return jax.shard_map(
        shards,
        mesh=mesh,
        in_specs=(
            P(None, "hidden", "width"),
            P("width"),
            P("width", "hidden"),
            P("width", "hidden"),
            P("hidden", "width"),
            P(("hidden", "width"), None, None),
            P(("hidden", "width"), None, None),
            P(("hidden", "width")),
        ),
        out_specs=P(None, "hidden", "width"),
        check_vma=False,
    )
```

```python
import jax
import jax.numpy as jnp
from jax import lax
from jax.experimental import pallas as pl
from jax.experimental.pallas import tpu as pltpu
from jax.sharding import PartitionSpec as P

MESH = pl.DeviceIdType.MESH
F32, BF16 = jnp.float32, jnp.bfloat16

D = 18432
HEADS = 48
HEAD_DIM = 256
CACHE = 2048
FEAT_DEV = 384
WIDTH_DEV = 1152
WIDTH_CHIP = 2304
JOINT = 512
EPS = 1e-05
MASKED_SCORE = -1e30

X, Y, Z = 4, 8, 8
BLOCK = WIDTH_DEV + 128
ORDER = (0, 1, 7, 2, 6, 3, 5, 4)
POS = {ry: pos for pos, ry in enumerate(ORDER)}
CHUNKS = ((0, 3), (3, 5), (5, 7), (7, 8))
BACK = ((0, 3, 0, 48), (3, 5, 48, 32), (5, 7, 80, 32), (7, 8, 112, 16))
STAT = 16

VMEM_BYTES = 55100 * 1024
ARRIVALS = 80
ARRIVAL_ORDER = (
    ("a", 0, 3), ("a", 0, 1), ("b", 7, 0), ("b", 1, 0), ("b", 0, 3), ("a", 0, 2),
    ("b", 6, 0), ("b", 2, 0), ("b", 0, 1), ("a", 7, 0), ("a", 1, 0), ("a", 7, 3),
    ("a", 1, 3), ("b", 7, 3), ("b", 7, 1), ("a", 7, 1), ("a", 1, 1), ("b", 1, 3),
    ("b", 1, 1), ("b", 0, 2), ("a", 7, 2), ("a", 1, 2), ("b", 6, 1), ("b", 6, 3),
    ("b", 5, 0), ("b", 3, 0), ("b", 2, 1), ("b", 2, 3), ("a", 6, 0), ("a", 2, 0),
    ("b", 7, 2), ("b", 1, 2), ("a", 6, 3), ("a", 2, 3), ("a", 6, 1), ("a", 2, 1),
    ("b", 6, 2), ("a", 6, 2), ("a", 2, 2), ("b", 5, 1), ("b", 5, 3), ("b", 4, 0),
    ("a", 3, 0), ("b", 3, 1), ("b", 3, 3), ("a", 5, 0), ("a", 3, 3), ("b", 2, 2),
    ("a", 5, 3), ("a", 3, 1), ("a", 5, 1), ("a", 3, 2), ("b", 5, 2), ("a", 5, 2),
    ("b", 4, 1), ("b", 4, 3), ("a", 4, 0), ("a", 4, 3), ("b", 4, 2), ("b", 3, 2),
    ("a", 4, 1), ("a", 4, 2),
)

RETURN_ORDER = (
    ("a", 4, 2), ("a", 4, 1), ("a", 4, 3), ("b", 4, 2), ("b", 4, 1), ("b", 4, 3),
    ("a", 4, 0), ("a", 5, 2), ("b", 3, 2), ("b", 5, 2), ("a", 3, 1), ("a", 5, 3),
    ("b", 3, 3), ("b", 5, 1), ("a", 3, 0), ("a", 3, 2), ("a", 5, 1), ("a", 3, 3),
    ("a", 5, 0), ("b", 4, 0), ("b", 2, 2), ("b", 6, 2), ("b", 2, 3), ("b", 6, 1),
    ("a", 6, 2), ("b", 3, 1), ("b", 5, 3), ("a", 2, 1), ("a", 6, 3), ("a", 2, 0),
    ("a", 6, 1), ("a", 2, 2), ("b", 1, 2), ("b", 7, 2), ("b", 0, 2), ("b", 1, 3),
    ("b", 7, 1), ("b", 0, 1), ("a", 6, 0), ("b", 2, 1), ("b", 6, 3), ("a", 2, 3),
    ("a", 1, 1), ("a", 7, 2), ("b", 3, 0), ("b", 5, 0), ("a", 1, 0), ("a", 7, 3),
    ("a", 1, 2), ("a", 7, 1), ("b", 1, 1), ("b", 7, 3), ("a", 7, 0), ("a", 1, 3),
    ("b", 0, 3), ("b", 2, 0), ("b", 6, 0), ("b", 1, 0), ("b", 7, 0), ("a", 0, 2),
    ("a", 0, 1), ("a", 0, 3),
)


def forwards(part, ry, rx):
    if part == "a":
        along = [(1, 0), (-1, 0)] if ry == 0 else []
        if ry >= 6 or (ry == 5 and rx < 2):
            along = [(1, 0)]
        if ry in (1, 2) or (ry == 3 and rx >= 2):
            along = [(-1, 0)]
        return ([(0, 1), (0, -1), (0, 2)] if (ry, rx) == (0, 0) else []) + along
    if rx == 0:
        along = {0: [(1, 0), (-1, 0), (2, 0), (-2, 0)], 6: [(1, 0)], 5: [(1, 0)], 2: [(-1, 0)]}.get(ry, [])
        return along + [(0, 1), (0, -1)] + ([(0, 2)] if ry == 4 else [])
    if ry != 4 and rx == (3 if POS[ry] % 2 == 0 else 1):
        return [(0, 1 if rx == 3 else -1)]
    return []


def reached(part, ry, rx):
    return [(dy, dx, (part, (ry - dy) % Y, (rx - dx) % X)) for dy, dx in forwards(part, ry, rx)]


BEFORE = {
    key: (-dy, -dx)
    for part in "ab"
    for ry in range(Y)
    for rx in range(X)
    for dy, dx, key in reached(part, ry, rx)
}

CROSSED = ((0, 1), (0, 3), (0, 2), (1, 0), (7, 0), (2, 0), (6, 0))


class Links:
    def __init__(self, send_sem, recv_sems):
        self.send_sem = send_sem
        self.recv_sems = recv_sems
        self.sent = []
        self.keys = {}
        self.devices = {}
        self.h = lax.axis_index("hidden")
        self.w = lax.axis_index("width")
        self.y, self.x = lax.div(self.h, X), lax.rem(self.h, X)
        self.z, self.c = lax.div(self.w, 2), lax.rem(self.w, 2)

    def hidden(self, ry, rx):
        return lax.rem(self.y + ry % Y, Y) * X + lax.rem(self.x + rx % X, X)

    def width(self, rz, rc):
        return lax.rem(self.z + rz % Z, Z) * 2 + self.core(rc)

    def core(self, rc):
        return self.c if rc == 0 else 1 - self.c

    def device(self, ry=0, rx=0, rz=0, rc=0, core=None):
        at = (ry % Y, rx % X, rz % Z, rc, core)
        if at not in self.devices:
            width = self.width(*at[2:4]) if core is None else self.z * 2 + core
            self.devices[at] = {"hidden": self.hidden(*at[:2]), "width": width}
        return self.devices[at]

    def arrival(self, key):
        return self.recv_sems.at[self.keys.setdefault(key, len(self.keys))]

    def copy(self, src, dst, to, key):
        return pltpu.make_async_remote_copy(
            src_ref=src,
            dst_ref=dst,
            send_sem=self.send_sem.at[0],
            recv_sem=self.arrival(key),
            device_id=self.device(**to),
            device_id_type=MESH,
        )

    def push(self, src, dst, to, key):
        copy = self.copy(src, dst, to, key)
        copy.start()
        self.sent.append(copy)

    def arrive(self, dst, key):
        pltpu.make_async_remote_copy(
            src_ref=dst,
            dst_ref=dst,
            send_sem=self.send_sem.at[0],
            recv_sem=self.arrival(key),
            device_id=self.device(rc=1),
            device_id_type=MESH,
        ).wait_recv()

    def finish(self):
        for copy in self.sent:
            copy.wait_send()


def iota(shape, axis):
    return lax.broadcasted_iota(jnp.int32, shape, axis)


def pieces(values):
    high = values.astype(BF16)
    rest = values - high.astype(F32)
    middle = rest.astype(BF16)
    return high, middle, (rest - middle.astype(F32)).astype(BF16)


def sum_all(terms):
    total = terms[0]
    for term in terms[1:]:
        total = total + term
    return total


def kernel(tokens, gain, lengths, query_weight, keyval_weight, out_weight, key_cache, value_cache, out, s):
    links = Links(s["send_sem"], s["recv_sems"])
    c, h, w = links.c, links.h, links.w
    width_peers = [(rz, rc) for rz in (4, 3, 5, 2, 6, 1, 7, 0) for rc in (0, 1) if (rz, rc) != (0, 0)]
    hidden_peers = [(ry, rx) for ry in reversed(ORDER) for rx in (2, 1, 3, 0) if (ry, rx) != (0, 0)]

    local = s["local_sems"]
    first_loads = [
        pltpu.make_async_copy(tokens, s["tokens"], local.at[5]),
        pltpu.make_async_copy(gain, s["gain"], local.at[6]),
    ]
    for load in first_loads:
        load.start()

    barrier = pltpu.get_barrier_semaphore()
    for rz, rc in width_peers:
        pl.semaphore_signal(barrier, inc=1, device_id=links.device(rz=rz, rc=rc), device_id_type=MESH)
    for ry, rx in hidden_peers:
        pl.semaphore_signal(barrier, inc=1, device_id=links.device(ry=ry, rx=rx), device_id_type=MESH)
    for ry, rx in CROSSED:
        pl.semaphore_signal(barrier, inc=1, device_id=links.device(ry=ry, rx=rx, rc=1), device_id_type=MESH)

    joint, out_w = s["joint"], s["out_w"]
    mine = pl.ds(pl.multiple_of(c * WIDTH_DEV, WIDTH_DEV), WIDTH_DEV)
    others = pl.ds(pl.multiple_of((1 - c) * WIDTH_DEV, WIDTH_DEV), WIDTH_DEV)
    loads = [
        pltpu.make_async_copy(keyval_weight, s["keyval_w"], local.at[0]),
        pltpu.make_async_copy(query_weight, joint.at[mine, pl.ds(0, FEAT_DEV)], local.at[1]),
        pltpu.make_async_copy(out_weight, out_w.at[c], local.at[2]),
        pltpu.make_async_copy(key_cache.at[0], s["keys"], local.at[3]),
        pltpu.make_async_copy(value_cache.at[0], s["values"], local.at[4]),
    ]
    for load in loads:
        load.start()

    for load in first_loads:
        load.wait()
    gain_row = s["gain"][...][None]
    rows = s["tokens"][...].astype(F32).reshape(32, WIDTH_DEV)
    own_mean = jnp.sum(rows, axis=1, keepdims=True) * (1.0 / WIDTH_DEV)
    centered = rows - own_mean
    own_spread = jnp.sum(centered * centered, axis=1, keepdims=True)
    lane = iota((32, 128), 1) - (STAT + 8 * c)
    lanes = jnp.zeros((32, 128), F32)
    for at, piece in enumerate(pieces(own_mean) + pieces(own_spread)):
        lanes = jnp.where(lane == at, piece.astype(F32), lanes)
    own_rows = s["own_rows"]
    own_rows[...] = jnp.concatenate([centered * gain_row, lanes], axis=1).astype(BF16).reshape(2, 16, BLOCK)

    block = {"a": s["ga"], "b": s["gb"]}
    parts = "ab"

    def first_copies(side):
        part = parts[side]
        to_other = [(0, 0, (part, 0, 0))]
        for step in (side, 1 - side):
            for dy, dx, key in reached(part, 0, 0) + (to_other if step != side else []):
                yield links.copy(
                    own_rows.at[step],
                    block[part].at[POS[key[1]], key[2]],
                    dict(ry=dy, rx=dx, core=step),
                    key if (dy, dx) != (0, 0) else "own chip",
                )

    for part in parts:
        for dy, dx, _ in reached(part, 0, 0) + [(0, 0, None)]:
            for step in (0, 1):
                links.device(ry=dy, rx=dx, core=step)

    pl.semaphore_wait(barrier, len(width_peers) + len(hidden_peers) + len(CROSSED))

    for side in (0, 1):

        @pl.when(c == side)
        def _(side=side):
            for copy in first_copies(side):
                copy.start()
            block[parts[side]][0, 0] = own_rows[side]

    def pass_on(part, ry, rx):
        for dy, dx, key in reached(part, ry, rx):
            links.push(
                block[part].at[POS[ry], rx], block[part].at[POS[key[1]], key[2]], dict(ry=dy, rx=dx), key
            )

    loads[0].wait()
    across = jnp.concatenate([s["keyval_w"][...].astype(F32), jnp.zeros((112, WIDTH_DEV), F32)], axis=0)
    joint[mine, FEAT_DEV:JOINT] = across.T.astype(BF16)
    loads[1].wait()
    links.push(joint.at[mine], joint.at[mine], dict(rc=1), "joint")
    eighth = iota((8, WIDTH_DEV), 0)
    gain_rows = jnp.zeros((8, WIDTH_DEV), F32)
    for at, piece in enumerate(pieces(gain_row)):
        gain_rows = jnp.where(eighth == at, piece.astype(F32), gain_rows)
    weight_sum = jnp.sum(
        jnp.dot(gain_rows.astype(BF16), joint[mine, :], preferred_element_type=F32), axis=0, keepdims=True
    )
    weight_sums = s["weight_sums"]
    eighth = iota((8, 128), 0)
    weight_tile = jnp.zeros((8, 128), F32)
    for k in range(4):
        weight_tile = jnp.where(eighth == k, weight_sum[:, k * 128 : (k + 1) * 128], weight_tile)
    weight_sums[c] = weight_tile
    for rz, rc in width_peers:
        links.push(weight_sums.at[c], weight_sums.at[((-rz) % Z) * 2 + c], dict(rz=rz, rc=rc), "weight_sums")
    loads[2].wait()
    links.push(out_w.at[c], out_w.at[c], dict(rc=1), "out_w")

    acc, spread_out, packed, shares = s["acc"], s["spread_out"], s["packed"], s["shares"]
    each, total, owned, queries = s["each"], s["total"], s["owned"], s["queries"]

    def project(chunk):
        p0, p1 = CHUNKS[chunk]
        count = p1 - p0
        if chunk == 0:
            links.arrive(joint.at[others], "joint")
            links.arrive(block["a"].at[0, 0], "own chip")
        sides = [block[part][p0:p1].reshape(count * 64, BLOCK) for part in parts]
        partial = sum_all(
            [
                jnp.dot(
                    rows_of[:, :WIDTH_DEV],
                    joint[side * WIDTH_DEV : (side + 1) * WIDTH_DEV],
                    preferred_element_type=F32,
                )
                for side, rows_of in enumerate(sides)
            ]
        )
        for k in range(3):
            acc[k, p0 * 64 : p1 * 64] = partial[:, k * 128 : (k + 1) * 128]
        acc[3, p0 * 64 : p1 * 64] = partial[:, FEAT_DEV:JOINT] + sum_all(
            [rows_of[:, WIDTH_DEV:].astype(F32) for rows_of in sides]
        )
        span = slice(p0 * 16, p1 * 16)
        for row in range(16):
            for k in range(4):
                spread_out[row, pl.ds(p0 * 16 + k, count * 4, stride=4), :] = acc[
                    k, pl.ds(p0 * 64 + row, count * 4, stride=16), :
                ]
            packed[row, span] = spread_out[row, span].astype(BF16)
        part = pl.ds(p0 * 16, count * 16)
        for rz, rc in width_peers:
            links.push(
                packed.at[links.width(rz, rc), part],
                shares.at[c * Z + (-rz) % Z, part],
                dict(rz=rz, rc=rc),
                ("shares", chunk),
            )
        shares[c * Z, span] = packed[w, span]

    def hand_out(chunk):
        p0, p1 = CHUNKS[chunk]
        count = (p1 - p0) * 4
        span = slice(p0 * 16, p1 * 16)
        links.arrive(shares.at[pl.ds(0, 15), pl.ds(p0 * 16, (p1 - p0) * 16)], ("shares", chunk))
        if chunk == 0:
            links.arrive(weight_sums.at[pl.ds(0, 15)], "weight_sums")
        lane = iota((count, 128), 1) - STAT

        def picked(values, chosen):
            return jnp.sum(jnp.where(chosen, values, 0.0), axis=1, keepdims=True)

        for step in range(2):
            terms = [shares[step * Z + rz, span].astype(F32) for rz in range(Z)]
            for rz in range(Z):
                each[rz, span] = terms[rz]
            total[span] = sum_all(terms)
            means = []
            for rz in range(Z):
                stats = each[rz, pl.ds(p0 * 16 + 3, count, stride=4), :]
                means += [picked(stats, (lane >= first) & (lane < first + 3)) for first in (0, 8)]
            spread = picked(
                total[pl.ds(p0 * 16 + 3, count, stride=4), :],
                ((lane >= 3) & (lane < 6)) | ((lane >= 11) & (lane < 14)),
            )
            mean = sum_all(means) * (1.0 / 16)
            apart = [own - mean for own in means]
            spread = spread + WIDTH_DEV * sum_all([gap * gap for gap in apart])
            scale = lax.rsqrt(spread * (1.0 / D) + EPS)
            for k in range(4):
                values = total[pl.ds(p0 * 16 + k, count, stride=4), :]
                for at, gap in enumerate(apart):
                    values = values + gap * weight_sums[at, k : k + 1, :]
                owned[pl.ds(p0 * 32 + step * 4 + k, count, stride=8), :] = values * scale
        here_h = pl.ds(pl.multiple_of(h * 8, 8), 8)
        for pos in range(p0, p1):
            ry = ORDER[pos]
            for rx in range(X):
                tile = pl.ds((pos * X + rx) * 8, 8)
                if (ry, rx) == (0, 0):
                    queries[here_h] = owned[tile]
                else:
                    links.push(owned.at[tile], queries.at[here_h], dict(ry=ry, rx=rx), "queries")

    missing = [{key for key in ARRIVAL_ORDER if p0 <= POS[key[1]] < p1} for p0, p1 in CHUNKS]
    for key in ARRIVAL_ORDER:
        part, ry, rx = key
        links.arrive(block[part].at[POS[ry], rx], key)
        pass_on(*key)
        for chunk in range(len(CHUNKS)):
            if key in missing[chunk]:
                missing[chunk].discard(key)
                if not missing[chunk]:
                    project(chunk)
    for chunk in range(len(CHUNKS)):
        hand_out(chunk)

    links.arrive(queries.at[pl.ds(0, 31 * 8)], "queries")
    blocks = s["blocks"]
    fresh = []
    lane_of = (iota((128, JOINT), 1) & 15) == iota((128, JOINT), 0)
    group_of = (iota((32, JOINT), 1) >> 4) == iota((32, JOINT), 0)
    for step in range(2):
        for k in range(3):
            blocks[pl.ds(step * 96 + k, 32, stride=3), :] = queries[pl.ds(step * 4 + k, 32, stride=8), :]
        keyval = queries[pl.ds(step * 4 + 3, 32, stride=8), :].astype(BF16)
        copies = jnp.dot(keyval, jnp.where(lane_of, 1.0, 0.0).astype(BF16), preferred_element_type=F32)
        fresh.append(jnp.sum(jnp.where(group_of, copies, 0.0), axis=0, keepdims=True))
    rows128 = iota((128, JOINT), 0)
    fresh_all = jnp.where(rows128 == 0, fresh[0], jnp.where(rows128 == 1, fresh[1], 0.0)).astype(BF16)
    query = jnp.concatenate(
        [
            jnp.concatenate(
                [blocks[pl.ds(step * 96 + half, 48, stride=2), :] for half in (0, 1)], axis=1
            )
            for step in range(2)
        ],
        axis=0,
    ).astype(BF16)
    inv_root = HEAD_DIM ** (-0.5)
    over_keys = (((1,), (1,)), ((), ()))
    loads[3].wait()
    cached = lax.dot_general(query, s["keys"][...], over_keys, preferred_element_type=F32) * inv_root
    cached = jnp.where(iota((96, CACHE), 1) < lengths[0], cached, MASKED_SCORE)
    new = lax.dot_general(query, fresh_all[:, :HEAD_DIM], over_keys, preferred_element_type=F32) * inv_root
    lane, row = iota((96, 128), 1), iota((96, 128), 0)
    new = jnp.where((lane == 0) | ((lane == 1) & (row >= HEADS)), new, MASKED_SCORE)
    peak = jnp.maximum(jnp.max(cached, axis=1, keepdims=True), jnp.max(new, axis=1, keepdims=True))
    cached = jnp.exp(cached - peak)
    new = jnp.exp(new - peak)
    total = jnp.sum(cached, axis=1, keepdims=True) + jnp.sum(new, axis=1, keepdims=True)
    loads[4].wait()
    weighted = jnp.dot(cached.astype(BF16), s["values"][...], preferred_element_type=F32) + jnp.dot(
        new.astype(BF16), fresh_all[:, HEAD_DIM:], preferred_element_type=F32
    )
    attended = (weighted / total).astype(BF16).astype(F32)

    att_blocks, leaving, landed = s["att_blocks"], s["leaving"], s["landed"]
    for step in range(2):
        for half in (0, 1):
            att_blocks[pl.ds(step * 96 + half, 48, stride=2), :] = attended[
                step * 48 : (step + 1) * 48, half * 128 : (half + 1) * 128
            ]
        for k in range(3):
            leaving[pl.ds(step * 4 + k, 32, stride=8), :] = att_blocks[pl.ds(step * 96 + k, 32, stride=3), :]
        leaving[pl.ds(step * 4 + 3, 32, stride=8), :] = jnp.zeros((32, 128), F32)

    def back_part(pos):
        return [part for part, (p0, p1, _, _) in enumerate(BACK) if p0 <= pos < p1][0]

    for ry, rx in hidden_peers:
        slot = POS[(-ry) % Y] * X + (-rx) % X
        links.push(
            leaving.at[pl.ds(pl.multiple_of(links.hidden(ry, rx) * 8, 8), 8)],
            landed.at[pl.ds(slot * 8, 8)],
            dict(ry=ry, rx=rx),
            ("landed", back_part(slot // X)),
        )
    landed[0:8] = leaving[pl.ds(pl.multiple_of(h * 8, 8), 8)]

    along_f32, along, whole, whole_f32 = s["along_f32"], s["along"], s["whole"], s["whole_f32"]
    feature_rows, product = s["feature_rows"], s["product"]

    def pass_along(part):
        p0, p1, first, held = BACK[part]
        count = (p1 - p0) * X
        span = slice(first, first + held)
        links.arrive(landed.at[pl.ds(p0 * 32, (count if p0 else count - 1) * 8)], ("landed", part))
        for step in range(2):
            for k in range(3):
                along_f32[step, pl.ds(first + k, count, stride=3), :] = landed[
                    pl.ds(p0 * 32 + step * 4 + k, count, stride=8), :
                ]
            if count * 3 < held:
                along_f32[step, first + count * 3 : first + held] = jnp.zeros((held - count * 3, 128), F32)
            along[step, span] = along_f32[step, span].astype(BF16)
        for rz, rc in width_peers:
            links.push(
                along.at[links.core(rc), pl.ds(first, held)],
                whole.at[w, pl.ds(first, held)],
                dict(rz=rz, rc=rc),
                ("whole", part),
            )
        whole[w, span] = along[c, span]

    def multiply(part):
        p0, p1, first, held = BACK[part]
        count = (p1 - p0) * X
        span = slice(first, first + held)
        links.arrive(whole.at[pl.ds(0, 15), pl.ds(first, held)], ("whole", part))
        for row in range(16):
            whole_f32[row, span] = whole[row, span].astype(F32)
            for k in range(3):
                feature_rows[k, pl.ds(p0 * 64 + row, count, stride=16), :] = whole_f32[
                    row, pl.ds(first + k, count, stride=3), :
                ]
        operand = jnp.concatenate([feature_rows[k, p0 * 64 : p1 * 64] for k in range(3)], axis=1).astype(BF16)
        for side in (0, 1):
            product[side, p0 * 64 : p1 * 64] = jnp.dot(operand, out_w[side], preferred_element_type=F32)

    for part in (3, 2, 1, 0):
        pass_along(part)
    links.arrive(out_w.at[1 - c], "out_w")

    staged = {"a": s["sa"], "b": s["sb"]}
    landing = {"a": s["la"], "b": s["lb"]}
    last, crossing = s["last"], s["crossing"]
    multiplied = set()

    def summed(part, ry, rx):
        back = back_part(POS[ry])
        if back not in multiplied:
            multiplied.add(back)
            multiply(back)
        at = (POS[ry] * X + rx) * 16
        terms = [product[parts.index(part), at : at + 16]]
        for _, _, key in reached(part, ry, rx):
            slot = landing[part].at[POS[key[1]], key[2]]
            links.arrive(slot, key)
            terms.append(slot[...].astype(F32))
        return sum_all(terms)

    for key in RETURN_ORDER:
        part, ry, rx = key
        at = (POS[ry], rx)
        staged[part][at] = summed(*key).astype(BF16)
        dy, dx = BEFORE[key]
        first_keys = [first_key for _, _, first_key in reached(part, 0, 0)]
        if key in first_keys:
            slot = 1 + 2 * first_keys.index(key) + c
            links.push(
                staged[part].at[at], last.at[slot], dict(ry=dy, rx=dx, core=parts.index(part)), "last"
            )
        else:
            links.push(staged[part].at[at], landing[part].at[at], dict(ry=dy, rx=dx), key)
    crossing[...] = product[1 - c, 0:16].astype(BF16)
    links.push(crossing, last.at[0], dict(rc=1), "last")

    for side in (0, 1):

        @pl.when(c == side)
        def _(side=side):
            count = len(reached(parts[side], 0, 0))
            links.arrive(last.at[pl.ds(0, 1 + 2 * count)], "last")
            for step in range(2):
                terms = [product[side, 0:16]] if step == side else [last[0].astype(F32)]
                terms += [last[1 + 2 * at + step].astype(F32) for at in range(count)]
                out[step] = sum_all(terms).astype(BF16)
            for copy in first_copies(side):
                copy.wait_send()

    links.finish()
    assert len(links.keys) <= ARRIVALS


SCRATCH = dict(
    tokens=((2, 16, WIDTH_DEV), BF16),
    gain=((WIDTH_DEV,), F32),
    own_rows=((2, 16, BLOCK), BF16),
    weight_sums=((16, 8, 128), F32),
    joint=((WIDTH_CHIP, JOINT), BF16),
    keyval_w=((16, WIDTH_DEV), BF16),
    out_w=((2, FEAT_DEV, WIDTH_DEV), BF16),
    keys=((CACHE, HEAD_DIM), BF16),
    values=((CACHE, HEAD_DIM), BF16),
    ga=((Y, X, 16, BLOCK), BF16),
    gb=((Y, X, 16, BLOCK), BF16),
    acc=((4, 512, 128), F32),
    spread_out=((16, 128, 128), F32),
    packed=((16, 128, 128), BF16),
    shares=((16, 128, 128), BF16),
    each=((Z, 128, 128), F32),
    total=((128, 128), F32),
    owned=((256, 128), F32),
    queries=((256, 128), F32),
    blocks=((192, 128), F32),
    att_blocks=((192, 128), F32),
    leaving=((256, 128), F32),
    landed=((256, 128), F32),
    along_f32=((2, 128, 128), F32),
    along=((2, 128, 128), BF16),
    whole=((16, 128, 128), BF16),
    whole_f32=((16, 128, 128), F32),
    feature_rows=((3, 512, 128), F32),
    product=((2, 512, WIDTH_DEV), F32),
    sa=((Y, X, 16, WIDTH_DEV), BF16),
    sb=((Y, X, 16, WIDTH_DEV), BF16),
    la=((Y, X, 16, WIDTH_DEV), BF16),
    lb=((Y, X, 16, WIDTH_DEV), BF16),
    last=((13, 16, WIDTH_DEV), BF16),
    crossing=((16, WIDTH_DEV), BF16),
)


def shards(tokens, gain, query_weight, keyval_weight, out_weight, key_cache, value_cache, lengths):
    names = list(SCRATCH)

    def body(*refs):
        scratch = dict(zip(names, refs[9:]))
        scratch.update(send_sem=refs[-3], recv_sems=refs[-2], local_sems=refs[-1])
        kernel(*refs[:9], scratch)

    vmem, smem, hbm = (pl.BlockSpec(memory_space=space) for space in (pltpu.VMEM, pltpu.SMEM, pl.ANY))
    return pl.pallas_call(
        body,
        out_shape=jax.ShapeDtypeStruct(tokens.shape, BF16),
        in_specs=[hbm, hbm, smem, hbm, hbm, hbm, hbm, hbm],
        out_specs=vmem,
        scratch_shapes=[pltpu.VMEM(shape, dtype) for shape, dtype in SCRATCH.values()]
        + [
            pltpu.SemaphoreType.DMA((1,)),
            pltpu.SemaphoreType.DMA((ARRIVALS,)),
            pltpu.SemaphoreType.DMA((7,)),
        ],
        compiler_params=pltpu.CompilerParams(
            collective_id=0, has_side_effects=True, vmem_limit_bytes=VMEM_BYTES
        ),
    )(tokens, gain, lengths, query_weight, keyval_weight.T, out_weight, key_cache, value_cache)


def solution(mesh):
    return jax.shard_map(
        shards,
        mesh=mesh,
        in_specs=(
            P(None, "hidden", "width"),
            P("width"),
            P("width", "hidden"),
            P("width", "hidden"),
            P("hidden", "width"),
            P(("hidden", "width"), None, None),
            P(("hidden", "width"), None, None),
            P(("hidden", "width")),
        ),
        out_specs=P(None, "hidden", "width"),
        check_vma=False,
    )
```

```python
import jax
import jax.numpy as jnp
from jax import lax
from jax.experimental import pallas as pl
from jax.experimental.pallas import tpu as pltpu
from jax.sharding import PartitionSpec as P

MESH = pl.DeviceIdType.MESH
F32, BF16 = jnp.float32, jnp.bfloat16

D = 18432
HEADS = 48
HEAD_DIM = 256
CACHE = 2048
FEAT_DEV = 384
WIDTH_DEV = 1152
WIDTH_CHIP = 2304
JOINT = 512
EPS = 1e-05
MASKED_SCORE = -1e30

X, Y, Z = 4, 8, 8
BLOCK = WIDTH_DEV + 128
ORDER = (0, 1, 7, 2, 6, 3, 5, 4)
POS = {ry: pos for pos, ry in enumerate(ORDER)}
CHUNKS = ((0, 1), (1, 3), (3, 5), (5, 7), (7, 8))
BACK = ((0, 1, 0, 16), (1, 3, 16, 32), (3, 5, 48, 32), (5, 7, 80, 32), (7, 8, 112, 16))
STAT = 16

VMEM_BYTES = 55100 * 1024
ARRIVALS = 84
ARRIVAL_ORDER = (
    ("a", 0, 3), ("a", 0, 1), ("b", 7, 0), ("b", 1, 0), ("b", 0, 3), ("a", 0, 2),
    ("b", 6, 0), ("b", 2, 0), ("b", 0, 1), ("a", 7, 0), ("a", 1, 0), ("a", 7, 3),
    ("a", 1, 3), ("b", 7, 3), ("b", 7, 1), ("a", 7, 1), ("a", 1, 1), ("b", 1, 3),
    ("b", 1, 1), ("b", 0, 2), ("a", 7, 2), ("a", 1, 2), ("b", 6, 1), ("b", 6, 3),
    ("b", 5, 0), ("b", 3, 0), ("b", 2, 1), ("b", 2, 3), ("a", 6, 0), ("a", 2, 0),
    ("b", 7, 2), ("b", 1, 2), ("a", 6, 3), ("a", 2, 3), ("a", 6, 1), ("a", 2, 1),
    ("b", 6, 2), ("a", 6, 2), ("a", 2, 2), ("b", 5, 1), ("b", 5, 3), ("b", 4, 0),
    ("a", 3, 0), ("b", 3, 1), ("b", 3, 3), ("a", 5, 0), ("a", 3, 3), ("b", 2, 2),
    ("a", 5, 3), ("a", 3, 1), ("a", 5, 1), ("a", 3, 2), ("b", 5, 2), ("a", 5, 2),
    ("b", 4, 1), ("b", 4, 3), ("a", 4, 0), ("a", 4, 3), ("b", 4, 2), ("b", 3, 2),
    ("a", 4, 1), ("a", 4, 2),
)

RETURN_ORDER = (
    ("a", 4, 2), ("a", 4, 1), ("a", 4, 3), ("b", 4, 2), ("b", 4, 1), ("b", 4, 3),
    ("a", 4, 0), ("a", 5, 2), ("b", 3, 2), ("b", 5, 2), ("a", 3, 1), ("a", 5, 3),
    ("b", 3, 3), ("b", 5, 1), ("a", 3, 0), ("a", 3, 2), ("a", 5, 1), ("a", 3, 3),
    ("a", 5, 0), ("b", 4, 0), ("b", 2, 2), ("b", 6, 2), ("b", 2, 3), ("b", 6, 1),
    ("a", 6, 2), ("b", 3, 1), ("b", 5, 3), ("a", 2, 1), ("a", 6, 3), ("a", 2, 0),
    ("b", 1, 2), ("b", 7, 2), ("b", 1, 3), ("b", 7, 1), ("a", 6, 1), ("a", 2, 2),
    ("b", 0, 2), ("b", 0, 1), ("a", 6, 0), ("b", 2, 1), ("b", 6, 3), ("a", 2, 3),
    ("a", 1, 1), ("a", 7, 2), ("b", 3, 0), ("b", 5, 0), ("a", 1, 0), ("a", 7, 3),
    ("b", 1, 1), ("b", 7, 3), ("a", 1, 2), ("a", 7, 1), ("a", 1, 3), ("a", 7, 0),
    ("b", 0, 3), ("b", 2, 0), ("b", 6, 0), ("b", 1, 0), ("b", 7, 0), ("a", 0, 2),
    ("a", 0, 1), ("a", 0, 3),
)


def forwards(part, ry, rx):
    if part == "a":
        along = [(1, 0), (-1, 0)] if ry == 0 else []
        if ry >= 6 or (ry == 5 and rx < 2):
            along = [(1, 0)]
        if ry in (1, 2) or (ry == 3 and rx >= 2):
            along = [(-1, 0)]
        return ([(0, 1), (0, -1), (0, 2)] if (ry, rx) == (0, 0) else []) + along
    if rx == 0:
        along = {0: [(1, 0), (-1, 0), (2, 0), (-2, 0)], 6: [(1, 0)], 5: [(1, 0)], 2: [(-1, 0)]}.get(ry, [])
        return along + [(0, 1), (0, -1)] + ([(0, 2)] if ry == 4 else [])
    if ry != 4 and rx == (3 if POS[ry] % 2 == 0 else 1):
        return [(0, 1 if rx == 3 else -1)]
    return []


def reached(part, ry, rx):
    return [(dy, dx, (part, (ry - dy) % Y, (rx - dx) % X)) for dy, dx in forwards(part, ry, rx)]


BEFORE = {
    key: (-dy, -dx)
    for part in "ab"
    for ry in range(Y)
    for rx in range(X)
    for dy, dx, key in reached(part, ry, rx)
}

NEAR = ((0, 1), (0, 3), (0, 2), (1, 0), (7, 0), (2, 0), (6, 0))


class Links:
    def __init__(self, send_sem, recv_sems):
        self.send_sem = send_sem
        self.recv_sems = recv_sems
        self.sent = []
        self.keys = {}
        self.devices = {}
        self.h = lax.axis_index("hidden")
        self.w = lax.axis_index("width")
        self.y, self.x = lax.div(self.h, X), lax.rem(self.h, X)
        self.z, self.c = lax.div(self.w, 2), lax.rem(self.w, 2)

    def hidden(self, ry, rx):
        return lax.rem(self.y + ry % Y, Y) * X + lax.rem(self.x + rx % X, X)

    def width(self, rz, rc):
        return lax.rem(self.z + rz % Z, Z) * 2 + self.core(rc)

    def core(self, rc):
        return self.c if rc == 0 else 1 - self.c

    def device(self, ry=0, rx=0, rz=0, rc=0, core=None):
        at = (ry % Y, rx % X, rz % Z, rc, core)
        if at not in self.devices:
            width = self.width(*at[2:4]) if core is None else self.z * 2 + core
            self.devices[at] = {"hidden": self.hidden(*at[:2]), "width": width}
        return self.devices[at]

    def arrival(self, key):
        return self.recv_sems.at[self.keys.setdefault(key, len(self.keys))]

    def copy(self, src, dst, to, key):
        return pltpu.make_async_remote_copy(
            src_ref=src,
            dst_ref=dst,
            send_sem=self.send_sem.at[0],
            recv_sem=self.arrival(key),
            device_id=self.device(**to),
            device_id_type=MESH,
        )

    def push(self, src, dst, to, key):
        copy = self.copy(src, dst, to, key)
        copy.start()
        self.sent.append(copy)

    def arrive(self, dst, key):
        pltpu.make_async_remote_copy(
            src_ref=dst,
            dst_ref=dst,
            send_sem=self.send_sem.at[0],
            recv_sem=self.arrival(key),
            device_id=self.device(rc=1),
            device_id_type=MESH,
        ).wait_recv()

    def finish(self):
        for copy in self.sent:
            copy.wait_send()


def iota(shape, axis):
    return lax.broadcasted_iota(jnp.int32, shape, axis)


def pieces(values):
    high = values.astype(BF16)
    rest = values - high.astype(F32)
    middle = rest.astype(BF16)
    return high, middle, (rest - middle.astype(F32)).astype(BF16)


def sum_all(terms):
    total = terms[0]
    for term in terms[1:]:
        total = total + term
    return total


def kernel(tokens, gain, lengths, query_weight, keyval_weight, out_weight, key_cache, value_cache, out, s):
    links = Links(s["send_sem"], s["recv_sems"])
    c, h, w = links.c, links.h, links.w
    width_peers = [(rz, rc) for rz in (4, 3, 5, 2, 6, 1, 7, 0) for rc in (0, 1) if (rz, rc) != (0, 0)]
    hidden_peers = [(ry, rx) for ry in reversed(ORDER) for rx in (2, 1, 3, 0) if (ry, rx) != (0, 0)]

    local = s["local_sems"]
    first_loads = [
        pltpu.make_async_copy(tokens, s["tokens"], local.at[5]),
        pltpu.make_async_copy(gain, s["gain"], local.at[6]),
    ]
    for load in first_loads:
        load.start()

    barrier = pltpu.get_barrier_semaphore()
    for rz, rc in width_peers:
        pl.semaphore_signal(barrier, inc=1, device_id=links.device(rz=rz, rc=rc), device_id_type=MESH)
    for ry, rx in NEAR:
        for rc in (0, 1):
            to = links.device(ry=ry, rx=rx, rc=rc)
            pl.semaphore_signal(barrier, inc=1, device_id=to, device_id_type=MESH)

    joint, out_w = s["joint"], s["out_w"]
    mine = pl.ds(pl.multiple_of(c * WIDTH_DEV, WIDTH_DEV), WIDTH_DEV)
    others = pl.ds(pl.multiple_of((1 - c) * WIDTH_DEV, WIDTH_DEV), WIDTH_DEV)
    loads = [
        pltpu.make_async_copy(keyval_weight, s["keyval_w"], local.at[0]),
        pltpu.make_async_copy(query_weight, joint.at[mine, pl.ds(0, FEAT_DEV)], local.at[1]),
        pltpu.make_async_copy(out_weight, out_w.at[c], local.at[2]),
        pltpu.make_async_copy(key_cache.at[0], s["keys"], local.at[3]),
        pltpu.make_async_copy(value_cache.at[0], s["values"], local.at[4]),
    ]
    for load in loads:
        load.start()

    for load in first_loads:
        load.wait()
    gain_row = s["gain"][...][None]
    rows = s["tokens"][...].astype(F32).reshape(32, WIDTH_DEV)
    own_mean = jnp.sum(rows, axis=1, keepdims=True) * (1.0 / WIDTH_DEV)
    centered = rows - own_mean
    own_spread = jnp.sum(centered * centered, axis=1, keepdims=True)
    lane = iota((32, 128), 1) - (STAT + 8 * c)
    lanes = jnp.zeros((32, 128), F32)
    for at, piece in enumerate(pieces(own_mean) + pieces(own_spread)):
        lanes = jnp.where(lane == at, piece.astype(F32), lanes)
    own_rows = s["own_rows"]
    own_rows[...] = jnp.concatenate([centered * gain_row, lanes], axis=1).astype(BF16).reshape(2, 16, BLOCK)

    block = {"a": s["ga"], "b": s["gb"]}
    parts = "ab"

    def first_copies(side):
        part = parts[side]
        to_other = [(0, 0, (part, 0, 0))]
        for step in (side, 1 - side):
            for dy, dx, key in reached(part, 0, 0) + (to_other if step != side else []):
                yield links.copy(
                    own_rows.at[step],
                    block[part].at[POS[key[1]], key[2]],
                    dict(ry=dy, rx=dx, core=step),
                    key if (dy, dx) != (0, 0) else "own chip",
                )

    for part in parts:
        for dy, dx, _ in reached(part, 0, 0) + [(0, 0, None)]:
            for step in (0, 1):
                links.device(ry=dy, rx=dx, core=step)

    pl.semaphore_wait(barrier, len(width_peers) + 2 * len(NEAR))

    for side in (0, 1):

        @pl.when(c == side)
        def _(side=side):
            for copy in first_copies(side):
                copy.start()
            block[parts[side]][0, 0] = own_rows[side]

    def pass_on(part, ry, rx):
        for dy, dx, key in reached(part, ry, rx):
            links.push(
                block[part].at[POS[ry], rx], block[part].at[POS[key[1]], key[2]], dict(ry=dy, rx=dx), key
            )

    loads[0].wait()
    across = jnp.concatenate([s["keyval_w"][...].astype(F32), jnp.zeros((112, WIDTH_DEV), F32)], axis=0)
    joint[mine, FEAT_DEV:JOINT] = across.T.astype(BF16)
    loads[1].wait()
    links.push(joint.at[mine], joint.at[mine], dict(rc=1), "joint")
    eighth = iota((8, WIDTH_DEV), 0)
    gain_rows = jnp.zeros((8, WIDTH_DEV), F32)
    for at, piece in enumerate(pieces(gain_row)):
        gain_rows = jnp.where(eighth == at, piece.astype(F32), gain_rows)
    weight_sum = jnp.sum(
        jnp.dot(gain_rows.astype(BF16), joint[mine, :], preferred_element_type=F32), axis=0, keepdims=True
    )
    weight_sums = s["weight_sums"]
    eighth = iota((8, 128), 0)
    weight_tile = jnp.zeros((8, 128), F32)
    for k in range(4):
        weight_tile = jnp.where(eighth == k, weight_sum[:, k * 128 : (k + 1) * 128], weight_tile)
    weight_sums[c] = weight_tile
    for rz, rc in width_peers:
        links.push(weight_sums.at[c], weight_sums.at[((-rz) % Z) * 2 + c], dict(rz=rz, rc=rc), "weight_sums")
    loads[2].wait()
    links.push(out_w.at[c], out_w.at[c], dict(rc=1), "out_w")

    acc, spread_out, packed, shares = s["acc"], s["spread_out"], s["packed"], s["shares"]
    each, total, owned, queries = s["each"], s["total"], s["owned"], s["queries"]

    def project(chunk):
        p0, p1 = CHUNKS[chunk]
        count = p1 - p0
        if chunk == 0:
            links.arrive(joint.at[others], "joint")
            links.arrive(block["a"].at[0, 0], "own chip")
        sides = [block[part][p0:p1].reshape(count * 64, BLOCK) for part in parts]
        partial = sum_all(
            [
                jnp.dot(
                    rows_of[:, :WIDTH_DEV],
                    joint[side * WIDTH_DEV : (side + 1) * WIDTH_DEV],
                    preferred_element_type=F32,
                )
                for side, rows_of in enumerate(sides)
            ]
        )
        for k in range(3):
            acc[k, p0 * 64 : p1 * 64] = partial[:, k * 128 : (k + 1) * 128]
        acc[3, p0 * 64 : p1 * 64] = partial[:, FEAT_DEV:JOINT] + sum_all(
            [rows_of[:, WIDTH_DEV:].astype(F32) for rows_of in sides]
        )
        span = slice(p0 * 16, p1 * 16)
        for row in range(16):
            for k in range(4):
                spread_out[row, pl.ds(p0 * 16 + k, count * 4, stride=4), :] = acc[
                    k, pl.ds(p0 * 64 + row, count * 4, stride=16), :
                ]
            packed[row, span] = spread_out[row, span].astype(BF16)
        part = pl.ds(p0 * 16, count * 16)
        for rz, rc in width_peers:
            links.push(
                packed.at[links.width(rz, rc), part],
                shares.at[c * Z + (-rz) % Z, part],
                dict(rz=rz, rc=rc),
                ("shares", chunk),
            )
        shares[c * Z, span] = packed[w, span]

    def hand_out(chunk):
        p0, p1 = CHUNKS[chunk]
        count = (p1 - p0) * 4
        span = slice(p0 * 16, p1 * 16)
        links.arrive(shares.at[pl.ds(0, 15), pl.ds(p0 * 16, (p1 - p0) * 16)], ("shares", chunk))
        if chunk == 0:
            links.arrive(weight_sums.at[pl.ds(0, 15)], "weight_sums")
        lane = iota((count, 128), 1) - STAT

        def picked(values, chosen):
            return jnp.sum(jnp.where(chosen, values, 0.0), axis=1, keepdims=True)

        for step in range(2):
            terms = [shares[step * Z + rz, span].astype(F32) for rz in range(Z)]
            for rz in range(Z):
                each[rz, span] = terms[rz]
            total[span] = sum_all(terms)
            means = []
            for rz in range(Z):
                stats = each[rz, pl.ds(p0 * 16 + 3, count, stride=4), :]
                means += [picked(stats, (lane >= first) & (lane < first + 3)) for first in (0, 8)]
            spread = picked(
                total[pl.ds(p0 * 16 + 3, count, stride=4), :],
                ((lane >= 3) & (lane < 6)) | ((lane >= 11) & (lane < 14)),
            )
            mean = sum_all(means) * (1.0 / 16)
            apart = [own - mean for own in means]
            spread = spread + WIDTH_DEV * sum_all([gap * gap for gap in apart])
            scale = lax.rsqrt(spread * (1.0 / D) + EPS)
            for k in range(4):
                values = total[pl.ds(p0 * 16 + k, count, stride=4), :]
                for at, gap in enumerate(apart):
                    values = values + gap * weight_sums[at, k : k + 1, :]
                owned[pl.ds(p0 * 32 + step * 4 + k, count, stride=8), :] = values * scale
        here_h = pl.ds(pl.multiple_of(h * 8, 8), 8)
        for pos in range(p0, p1):
            ry = ORDER[pos]
            for rx in range(X):
                tile = pl.ds((pos * X + rx) * 8, 8)
                if (ry, rx) == (0, 0):
                    queries[here_h] = owned[tile]
                else:
                    links.push(owned.at[tile], queries.at[here_h], dict(ry=ry, rx=rx), "queries")

    missing = [{key for key in ARRIVAL_ORDER if p0 <= POS[key[1]] < p1} for p0, p1 in CHUNKS]
    for key in ARRIVAL_ORDER:
        part, ry, rx = key
        links.arrive(block[part].at[POS[ry], rx], key)
        pass_on(*key)
        for chunk in range(len(CHUNKS)):
            if key in missing[chunk]:
                missing[chunk].discard(key)
                if not missing[chunk]:
                    project(chunk)
    for chunk in range(len(CHUNKS)):
        hand_out(chunk)

    links.arrive(queries.at[pl.ds(0, 31 * 8)], "queries")
    blocks = s["blocks"]
    fresh = []
    lane_of = (iota((128, JOINT), 1) & 15) == iota((128, JOINT), 0)
    group_of = (iota((32, JOINT), 1) >> 4) == iota((32, JOINT), 0)
    for step in range(2):
        for k in range(3):
            blocks[pl.ds(step * 96 + k, 32, stride=3), :] = queries[pl.ds(step * 4 + k, 32, stride=8), :]
        keyval = queries[pl.ds(step * 4 + 3, 32, stride=8), :].astype(BF16)
        copies = jnp.dot(keyval, jnp.where(lane_of, 1.0, 0.0).astype(BF16), preferred_element_type=F32)
        fresh.append(jnp.sum(jnp.where(group_of, copies, 0.0), axis=0, keepdims=True))
    rows128 = iota((128, JOINT), 0)
    fresh_all = jnp.where(rows128 == 0, fresh[0], jnp.where(rows128 == 1, fresh[1], 0.0)).astype(BF16)
    query = jnp.concatenate(
        [
            jnp.concatenate(
                [blocks[pl.ds(step * 96 + half, 48, stride=2), :] for half in (0, 1)], axis=1
            )
            for step in range(2)
        ],
        axis=0,
    ).astype(BF16)
    inv_root = HEAD_DIM ** (-0.5)
    over_keys = (((1,), (1,)), ((), ()))
    loads[3].wait()
    cached = lax.dot_general(query, s["keys"][...], over_keys, preferred_element_type=F32) * inv_root
    cached = jnp.where(iota((96, CACHE), 1) < lengths[0], cached, MASKED_SCORE)
    new = lax.dot_general(query, fresh_all[:, :HEAD_DIM], over_keys, preferred_element_type=F32) * inv_root
    lane, row = iota((96, 128), 1), iota((96, 128), 0)
    new = jnp.where((lane == 0) | ((lane == 1) & (row >= HEADS)), new, MASKED_SCORE)
    peak = jnp.maximum(jnp.max(cached, axis=1, keepdims=True), jnp.max(new, axis=1, keepdims=True))
    cached = jnp.exp(cached - peak)
    new = jnp.exp(new - peak)
    total = jnp.sum(cached, axis=1, keepdims=True) + jnp.sum(new, axis=1, keepdims=True)
    loads[4].wait()
    weighted = jnp.dot(cached.astype(BF16), s["values"][...], preferred_element_type=F32) + jnp.dot(
        new.astype(BF16), fresh_all[:, HEAD_DIM:], preferred_element_type=F32
    )
    attended = (weighted / total).astype(BF16).astype(F32)

    att_blocks, leaving, landed = s["att_blocks"], s["leaving"], s["landed"]
    for step in range(2):
        for half in (0, 1):
            att_blocks[pl.ds(step * 96 + half, 48, stride=2), :] = attended[
                step * 48 : (step + 1) * 48, half * 128 : (half + 1) * 128
            ]
        for k in range(3):
            leaving[pl.ds(step * 4 + k, 32, stride=8), :] = att_blocks[pl.ds(step * 96 + k, 32, stride=3), :]
        leaving[pl.ds(step * 4 + 3, 32, stride=8), :] = jnp.zeros((32, 128), F32)

    def back_part(pos):
        return [part for part, (p0, p1, _, _) in enumerate(BACK) if p0 <= pos < p1][0]

    for ry, rx in hidden_peers:
        slot = POS[(-ry) % Y] * X + (-rx) % X
        links.push(
            leaving.at[pl.ds(pl.multiple_of(links.hidden(ry, rx) * 8, 8), 8)],
            landed.at[pl.ds(slot * 8, 8)],
            dict(ry=ry, rx=rx),
            ("landed", back_part(slot // X)),
        )
    landed[0:8] = leaving[pl.ds(pl.multiple_of(h * 8, 8), 8)]

    along_f32, along, whole, whole_f32 = s["along_f32"], s["along"], s["whole"], s["whole_f32"]
    feature_rows, product = s["feature_rows"], s["product"]

    def pass_along(part):
        p0, p1, first, held = BACK[part]
        count = (p1 - p0) * X
        span = slice(first, first + held)
        links.arrive(landed.at[pl.ds(p0 * 32, (count if p0 else count - 1) * 8)], ("landed", part))
        for step in range(2):
            for k in range(3):
                along_f32[step, pl.ds(first + k, count, stride=3), :] = landed[
                    pl.ds(p0 * 32 + step * 4 + k, count, stride=8), :
                ]
            if count * 3 < held:
                along_f32[step, first + count * 3 : first + held] = jnp.zeros((held - count * 3, 128), F32)
            along[step, span] = along_f32[step, span].astype(BF16)
        for rz, rc in width_peers:
            links.push(
                along.at[links.core(rc), pl.ds(first, held)],
                whole.at[w, pl.ds(first, held)],
                dict(rz=rz, rc=rc),
                ("whole", part),
            )
        whole[w, span] = along[c, span]

    def multiply(part):
        p0, p1, first, held = BACK[part]
        count = (p1 - p0) * X
        span = slice(first, first + held)
        links.arrive(whole.at[pl.ds(0, 15), pl.ds(first, held)], ("whole", part))
        for row in range(16):
            whole_f32[row, span] = whole[row, span].astype(F32)
            for k in range(3):
                feature_rows[k, pl.ds(p0 * 64 + row, count, stride=16), :] = whole_f32[
                    row, pl.ds(first + k, count, stride=3), :
                ]
        operand = jnp.concatenate([feature_rows[k, p0 * 64 : p1 * 64] for k in range(3)], axis=1).astype(BF16)
        for side in (0, 1):
            product[side, p0 * 64 : p1 * 64] = jnp.dot(operand, out_w[side], preferred_element_type=F32)

    for part in (4, 3, 2, 1, 0):
        pass_along(part)
    links.arrive(out_w.at[1 - c], "out_w")

    staged = {"a": s["sa"], "b": s["sb"]}
    landing = {"a": s["la"], "b": s["lb"]}
    last, crossing = s["last"], s["crossing"]
    multiplied = set()

    def summed(part, ry, rx):
        back = back_part(POS[ry])
        if back not in multiplied:
            multiplied.add(back)
            multiply(back)
        at = (POS[ry] * X + rx) * 16
        terms = [product[parts.index(part), at : at + 16]]
        for _, _, key in reached(part, ry, rx):
            slot = landing[part].at[POS[key[1]], key[2]]
            links.arrive(slot, key)
            terms.append(slot[...].astype(F32))
        return sum_all(terms)

    for key in RETURN_ORDER:
        part, ry, rx = key
        at = (POS[ry], rx)
        staged[part][at] = summed(*key).astype(BF16)
        dy, dx = BEFORE[key]
        first_keys = [first_key for _, _, first_key in reached(part, 0, 0)]
        if key in first_keys:
            slot = 1 + 2 * first_keys.index(key) + c
            links.push(
                staged[part].at[at], last.at[slot], dict(ry=dy, rx=dx, core=parts.index(part)), "last"
            )
        else:
            links.push(staged[part].at[at], landing[part].at[at], dict(ry=dy, rx=dx), key)
    crossing[...] = product[1 - c, 0:16].astype(BF16)
    links.push(crossing, last.at[0], dict(rc=1), "last")

    for side in (0, 1):

        @pl.when(c == side)
        def _(side=side):
            count = len(reached(parts[side], 0, 0))
            links.arrive(last.at[pl.ds(0, 1 + 2 * count)], "last")
            for step in range(2):
                terms = [product[side, 0:16]] if step == side else [last[0].astype(F32)]
                terms += [last[1 + 2 * at + step].astype(F32) for at in range(count)]
                out[step] = sum_all(terms).astype(BF16)
            for copy in first_copies(side):
                copy.wait_send()

    links.finish()
    assert len(links.keys) <= ARRIVALS


SCRATCH = dict(
    tokens=((2, 16, WIDTH_DEV), BF16),
    gain=((WIDTH_DEV,), F32),
    own_rows=((2, 16, BLOCK), BF16),
    weight_sums=((16, 8, 128), F32),
    joint=((WIDTH_CHIP, JOINT), BF16),
    keyval_w=((16, WIDTH_DEV), BF16),
    out_w=((2, FEAT_DEV, WIDTH_DEV), BF16),
    keys=((CACHE, HEAD_DIM), BF16),
    values=((CACHE, HEAD_DIM), BF16),
    ga=((Y, X, 16, BLOCK), BF16),
    gb=((Y, X, 16, BLOCK), BF16),
    acc=((4, 512, 128), F32),
    spread_out=((16, 128, 128), F32),
    packed=((16, 128, 128), BF16),
    shares=((16, 128, 128), BF16),
    each=((Z, 128, 128), F32),
    total=((128, 128), F32),
    owned=((256, 128), F32),
    queries=((256, 128), F32),
    blocks=((192, 128), F32),
    att_blocks=((192, 128), F32),
    leaving=((256, 128), F32),
    landed=((256, 128), F32),
    along_f32=((2, 128, 128), F32),
    along=((2, 128, 128), BF16),
    whole=((16, 128, 128), BF16),
    whole_f32=((16, 128, 128), F32),
    feature_rows=((3, 512, 128), F32),
    product=((2, 512, WIDTH_DEV), F32),
    sa=((Y, X, 16, WIDTH_DEV), BF16),
    sb=((Y, X, 16, WIDTH_DEV), BF16),
    la=((Y, X, 16, WIDTH_DEV), BF16),
    lb=((Y, X, 16, WIDTH_DEV), BF16),
    last=((13, 16, WIDTH_DEV), BF16),
    crossing=((16, WIDTH_DEV), BF16),
)


def shards(tokens, gain, query_weight, keyval_weight, out_weight, key_cache, value_cache, lengths):
    names = list(SCRATCH)

    def body(*refs):
        scratch = dict(zip(names, refs[9:]))
        scratch.update(send_sem=refs[-3], recv_sems=refs[-2], local_sems=refs[-1])
        kernel(*refs[:9], scratch)

    vmem, smem, hbm = (pl.BlockSpec(memory_space=space) for space in (pltpu.VMEM, pltpu.SMEM, pltpu.HBM))
    return pl.pallas_call(
        body,
        out_shape=jax.ShapeDtypeStruct(tokens.shape, BF16),
        in_specs=[hbm, hbm, smem, hbm, hbm, hbm, hbm, hbm],
        out_specs=vmem,
        scratch_shapes=[pltpu.VMEM(shape, dtype) for shape, dtype in SCRATCH.values()]
        + [
            pltpu.SemaphoreType.DMA((1,)),
            pltpu.SemaphoreType.DMA((ARRIVALS,)),
            pltpu.SemaphoreType.DMA((7,)),
        ],
        compiler_params=pltpu.CompilerParams(
            collective_id=0, has_side_effects=True, vmem_limit_bytes=VMEM_BYTES
        ),
    )(tokens, gain, lengths, query_weight, keyval_weight.T, out_weight, key_cache, value_cache)


def solution(mesh):
    return jax.shard_map(
        shards,
        mesh=mesh,
        in_specs=(
            P(None, "hidden", "width"),
            P("width"),
            P("width", "hidden"),
            P("width", "hidden"),
            P("hidden", "width"),
            P(("hidden", "width"), None, None),
            P(("hidden", "width"), None, None),
            P(("hidden", "width")),
        ),
        out_specs=P(None, "hidden", "width"),
        check_vma=False,
    )
```
